256 devices in a mesh: dp: 16 (over y_hi, x, core), tensor: 16 (over z, y_lo).
Axes of the slice: x: 4, y: 4 (y_hi: 2, y_lo: 2; y = y_hi * 2 + y_lo), z: 8, core: 2. Of those that a mesh axis runs over, the one named last changes fastest.
Arguments:
- inputs: bfloat16 [8192, 4096], P(('dp', 'tensor')), may hold values from -6 to 6
- cotangent: bfloat16 [8192, 4096], P(('dp', 'tensor')), may hold values from -6 to 6
- gate_up: bfloat16 [2, 8192, 14336], P(None, 'dp', 'tensor'), may hold values from -6 to 6
- down_weight: bfloat16 [14336, 4096], P('tensor'), may hold values from -0.046875 to 0.046875
- proj_model: bfloat16 [4096, 192], replicated
- proj_hidden: bfloat16 [14336, 192], P('tensor')
- lengths: int32 [16], P('dp'), may hold values from 128 to 512
- queries: bfloat16 [256, 12288], P('dp'), may hold values from -6 to 6
Outputs:
- scores: float32 [16, 256], P('dp')
The draws below stay inside these ranges and needn't reach their ends.
All inputs are finite; a program needn't handle non-finite values.
Results may differ from the reference program's by a relative error of at most 0.0043.
Values may be sent and summed in bfloat16 or wider, within the bound.
A program may use at most 64 MiB of HBM per device.

```python
import jax
import jax.numpy as jnp
from jax import lax

D = 4096
FF = 14336
RANK = 64
LEN = 512
QUERIES = 256
EXAMPLES = 16
TOKENS = 8192


def draw_proj_model(key, part):
    key = jax.random.fold_in(key, 11)
    first, second = jax.random.split(key)
    base = jax.random.normal(first, (D, 3 * RANK), jnp.float32)
    top = 10.0
    scales = jnp.exp(jax.random.uniform(second, (1, 3 * RANK), jnp.float32) * jnp.log(top))
    return (base * scales * D ** (-0.5)).astype(jnp.bfloat16)


def draw_proj_hidden(key, part):
    key = jax.random.fold_in(key, 12)
    first, second = jax.random.split(key)
    base = jax.random.normal(first, (FF, 3 * RANK), jnp.float32)
    top = 10.0
    scales = jnp.exp(jax.random.uniform(second, (1, 3 * RANK), jnp.float32) * jnp.log(top))
    return (base * scales * FF ** (-0.5)).astype(jnp.bfloat16)


def plant(drawn, rng, least, top_value):
    longest = drawn.shape.index(max(drawn.shape))
    spots = []
    for shift in (0, 1):
        where = [jax.random.randint(jax.random.fold_in(rng, axis), (), 0, length) for axis, length in enumerate(drawn.shape)]
        where[longest] = (where[longest] + shift) % drawn.shape[longest]
        spots.append(tuple(where))
    return drawn.at[spots[0]].set(least).at[spots[1]].set(top_value)


def steps_of(own_key, dims, pieces, least, largest):
    def one(dim, shards_of):
        steps = jax.random.uniform(jax.random.fold_in(jax.random.fold_in(own_key, 6), dim), (shards_of,), jnp.float32, least / len(pieces), largest / len(pieces))
        return jnp.repeat(jnp.exp(steps), dims[dim] // shards_of).reshape((-1,) + (1,) * (len(dims) - dim - 1))

    gain = one(*pieces[0])
    for cut in pieces[1:]:
        gain = gain * one(*cut)
    return gain


def gaussian(key, dims, spread, limit, shards=(), kind=jnp.bfloat16):
    factor_of = steps_of(key, dims, shards, -0.22, 0.18) if shards else 1.0
    result = jax.random.normal(key, dims, jnp.float32) * spread * factor_of
    return jnp.minimum(jnp.maximum(result, -limit), limit).astype(kind)


def setup_inputs(seed: int = 0) -> dict:
    splits = jax.random.split(jax.random.key(seed), 9)
    inputs = gaussian(splits[0], (TOKENS, D), 1.0, 6.0, ((0, 256),))
    cotangent = gaussian(splits[1], (TOKENS, D), 1.0, 6.0, ((0, 256),))
    gate_up = gaussian(splits[2], (2, TOKENS, FF), 1.0, 6.0, ((1, 16), (2, 16)))
    down_weight = gaussian(splits[3], (FF, D), FF ** -0.5, 0.046875, ((0, 16),))
    proj_model = draw_proj_model(jax.random.fold_in(splits[8], 71), 0)
    proj_hidden = draw_proj_hidden(jax.random.fold_in(splits[8], 71), 0)
    lengths = plant(jax.random.randint(splits[6], (EXAMPLES,), LEN // 4, LEN + 1), jax.random.fold_in(splits[6], 1), LEN // 4, LEN).astype(jnp.int32)
    queries = gaussian(splits[7], (QUERIES, 3 * RANK * RANK), 1.0, 6.0, ((0, 16),))
    return dict(inputs=inputs, cotangent=cotangent, gate_up=gate_up, down_weight=down_weight, proj_model=proj_model, proj_hidden=proj_hidden, lengths=lengths, queries=queries)


def local_terms(grad_hidden, gate_pre, up_value):
    gate_pre = gate_pre.astype(jnp.float32)
    up_value = up_value.astype(jnp.float32)
    sigma = jax.nn.sigmoid(gate_pre)
    silu_gate = gate_pre * sigma
    hidden = (silu_gate * up_value).astype(jnp.bfloat16)
    grad_up = (grad_hidden * silu_gate).astype(jnp.bfloat16)
    grad_gate = (grad_hidden * up_value * sigma * (1.0 + gate_pre * (1.0 - sigma))).astype(jnp.bfloat16)
    return (grad_gate, grad_up, hidden)

def project_hidden(parts, proj_hidden):
    columns = []
    for index in range(3):
        block = proj_hidden[:, index * RANK:(index + 1) * RANK]
        columns.append(jnp.dot(parts[index], block, preferred_element_type=jnp.float32))
    return jnp.concatenate(columns, axis=1)

def project_model(inputs, cotangent, proj_model):
    first = jnp.dot(inputs, proj_model[:, :2 * RANK], preferred_element_type=jnp.float32)
    second = jnp.dot(cotangent, proj_model[:, 2 * RANK:], preferred_element_type=jnp.float32)
    return jnp.concatenate([first, second], axis=1)

def sketch(weights, model_side, hidden_side):
    inward = (model_side[:, :RANK], model_side[:, RANK:2 * RANK], hidden_side[:, 2 * RANK:])
    outward = (hidden_side[:, :RANK], hidden_side[:, RANK:2 * RANK], model_side[:, 2 * RANK:])
    blocks = []
    for source, target in zip(inward, outward):
        scaled = weights[:, :, None] * source[:, None, :]
        blocks.append(jnp.einsum('tei,tj->eij', scaled, target, precision=lax.Precision.HIGHEST))
    stacked = jnp.stack(blocks, axis=1)
    return stacked.reshape(stacked.shape[0], 3 * RANK * RANK)

def reference(inputs, cotangent, gate_up, down_weight, proj_model, proj_hidden, lengths, queries):

    def one_example(example):
        first = (example * LEN).astype(jnp.int32)
        x_rows = lax.dynamic_slice_in_dim(inputs, first, LEN, 0)
        grad_rows = lax.dynamic_slice_in_dim(cotangent, first, LEN, 0)
        gate_rows = lax.dynamic_slice_in_dim(gate_up[0], first, LEN, 0)
        up_rows = lax.dynamic_slice_in_dim(gate_up[1], first, LEN, 0)
        grad_hidden = lax.dot_general(grad_rows, down_weight, (((1,), (1,)), ((), ())), preferred_element_type=jnp.float32)
        parts = local_terms(grad_hidden, gate_rows, up_rows)
        hidden_side = project_hidden(parts, proj_hidden)
        model_side = project_model(x_rows, grad_rows, proj_model)
        live = (jnp.arange(LEN, dtype=jnp.int32) < lengths[example]).astype(jnp.float32)
        return sketch(live[:, None], model_side, hidden_side)[0]
    sketches = lax.map(one_example, jnp.arange(EXAMPLES, dtype=jnp.int32))
    norms = jnp.sqrt(lax.optimization_barrier(jnp.sum(sketches * sketches, axis=1)) + 1e-06)
    unit = (sketches / norms[:, None]).astype(jnp.bfloat16)
    return lax.dot_general(unit, queries, (((1,), (1,)), ((), ())), preferred_element_type=jnp.float32)
```

```python
import jax
import jax.numpy as jnp
from jax import lax
from jax.experimental import pallas as pl
from jax.experimental.pallas import tpu as pltpu
from jax.sharding import PartitionSpec as P

MESH = pl.DeviceIdType.MESH
RANK = 64
N = 16
STEPS = 5
PIECES = 2
D = 4096
FF = 896
ROWS = 32
WIDE = D + 2 * RANK
SLICE = 768
CUTS = tuple((D // PIECES * j, D // PIECES * (j + 1)) for j in range(PIECES))
NT = (((1,), (1,)), ((), ()))
TN = (((0,), (0,)), ((), ()))

DOWN, UP, ACROSS = 0, 1, 2


def span(piece):
    low, high = CUTS[piece]
    return pl.ds(low, (WIDE if piece == PIECES - 1 else high) - low)


def slot_of(step, link):
    return 1 + 3 * (step - 1) + link


def dot(a, b, dims):
    return lax.dot_general(a, b, dims, preferred_element_type=jnp.float32)


def kernel(
    lengths,
    inputs,
    cotangent,
    gate_up,
    down_weight,
    proj_model,
    proj_hidden,
    queries,
    out,
    block,
    weight,
    gates,
    factor_up,
    factor_gate,
    x_rows,
    pm,
    ph,
    hidden_proj,
    grad,
    model_cot,
    total,
    turned,
    parts,
    parts_in,
    query_in,
    tile,
    tiles_in,
    load_sem,
    gate_sem,
    send_sem,
    recv_sem,
    query_send,
    query_recv,
    parts_send,
    parts_recv,
    tile_send,
    tile_recv,
):
    dp = lax.axis_index("dp")
    me = lax.axis_index("tensor")
    z, b = me // 2, me % 2
    z_down, z_up = (z + 7) % 8, (z + 1) % 8
    partner = me + 1 - 2 * b
    target = {DOWN: z_up * 2 + b, UP: z_down * 2 + b, ACROSS: partner}

    def query_peer(r):
        d = (dp + r) % N
        other = (d // 8 + dp // 8) % 2
        return d, me + other * (1 - 2 * b)

    owners = [me]
    same = lambda d: ((z + d + 8) % 8) * 2 + b
    opposite = lambda d: ((z + d + 8) % 8) * 2 + 1 - b
    for trio in (
        (same(-1), same(1), opposite(0)),
        (same(-2), same(2), opposite(1)),
        (same(-3), same(3), opposite(2)),
        (same(-4), opposite(3), opposite(-2)),
        (opposite(-3), opposite(4), opposite(-1)),
    ):
        owners += trio

    load_x = pltpu.make_async_copy(inputs, x_rows, load_sem.at[0])
    load_pm = pltpu.make_async_copy(proj_model, pm, load_sem.at[1])
    load_own = pltpu.make_async_copy(cotangent, block.at[0, :, pl.ds(0, D)], load_sem.at[2])
    load_ph = pltpu.make_async_copy(proj_hidden, ph, load_sem.at[3])
    load_query = pltpu.make_async_copy(
        queries.at[:, pl.ds(pl.multiple_of(me * SLICE, 128), SLICE)],
        query_in.at[dp],
        load_sem.at[4],
    )
    load_weight = [
        pltpu.make_async_copy(
            down_weight.at[:, pl.ds(low, high - low)],
            weight.at[:, pl.ds(low, high - low)],
            load_sem.at[5 + j],
        )
        for j, (low, high) in enumerate(CUTS)
    ]
    load_gates = [
        pltpu.make_async_copy(
            gate_up.at[:, pl.ds(pl.multiple_of(owner * ROWS, ROWS), ROWS), :],
            gates.at[:, pl.ds(slot * ROWS, ROWS), :],
            gate_sem.at[slot],
        )
        for slot, owner in enumerate(owners)
    ]
    load_x.start()
    load_pm.start()
    load_own.start()
    load_ph.start()
    for copy in load_gates:
        copy.start()
    for copy in load_weight:
        copy.start()
    load_query.start()

    barrier = pltpu.get_barrier_semaphore()

    def greet(r, carry):
        pl.semaphore_signal(
            barrier, inc=1, device_id=(dp, (me + r) % N), device_id_type=MESH
        )
        pl.semaphore_signal(barrier, inc=1, device_id=query_peer(r), device_id_type=MESH)
        return carry

    lax.fori_loop(1, N, greet, 0)
    pl.semaphore_wait(barrier, 2 * (N - 1))

    def pass_on(step, link, piece, source=None):
        where = block.at[slot_of(step, link), :, span(piece)]
        return pltpu.make_async_remote_copy(
            src_ref=where if source is None else source,
            dst_ref=where,
            send_sem=send_sem.at[link, step - 1, piece],
            recv_sem=recv_sem.at[link, step - 1, piece],
            device_id=(dp, target[link]),
            device_id_type=MESH,
        )

    sent = []

    def send(step, link, piece, source_slot):
        copy = pass_on(step, link, piece, block.at[source_slot, :, span(piece)])
        copy.start()
        sent.append(copy)

    for link in (DOWN, UP, ACROSS):
        for piece in range(PIECES - 1):
            copy = pass_on(1, link, piece, cotangent.at[:, span(piece)])
            copy.start()
            sent.append(copy)

    load_x.wait()
    load_pm.wait()
    lead = dot(x_rows[...], pm[:, : 2 * RANK], (((1,), (0,)), ((), ())))
    load_own.wait()
    block[0, :, D:] = lead.astype(jnp.bfloat16)
    for link in (DOWN, UP, ACROSS):
        send(1, link, PIECES - 1, 0)

    def query_copy(r):
        d, tensor = query_peer(r)
        return pltpu.make_async_remote_copy(
            src_ref=queries.at[:, pl.ds(pl.multiple_of(tensor * SLICE, 128), SLICE)],
            dst_ref=query_in.at[dp],
            send_sem=query_send.at[r],
            recv_sem=query_recv.at[dp],
            device_id=(d, tensor),
            device_id_type=MESH,
        )

    def start_query(r, carry):
        query_copy(r).start()
        return carry

    lax.fori_loop(1, N, start_query, 0)

    load_ph.wait()
    for copy in load_gates:
        copy.wait()

    def gate_rows(i, carry):
        rows = pl.ds(pl.multiple_of(i * ROWS, ROWS), ROWS)
        g = gates[0, rows, :].astype(jnp.float32)
        u = gates[1, rows, :].astype(jnp.float32)
        s = jax.nn.sigmoid(g)
        silu = g * s
        factor_up[rows, :] = silu
        factor_gate[rows, :] = u * s * (1.0 + g * (1.0 - s))
        hidden = (silu * u).astype(jnp.bfloat16)
        hidden_proj[rows, :] = dot(hidden, ph[...], (((1,), (0,)), ((), ())))
        return carry

    lax.fori_loop(0, N, gate_rows, 0)
    total[...] = jnp.zeros_like(total)
    parts[...] = jnp.zeros_like(parts)

    live_count = lengths[0]

    def multiply(first, count, piece):
        low, high = CUTS[piece]
        rows = count * ROWS
        x = block[first : first + count, :, low:high].reshape(rows, high - low)
        for n in range(0, FF, 256):
            m = min(n + 256, FF)
            term = dot(x, weight[n:m, low:high], NT)
            if piece:
                term += grad[:rows, n:m]
            grad[:rows, n:m] = term
        term = dot(x, pm[low:high, :], (((1,), (0,)), ((), ())))
        if piece:
            term += model_cot[:rows, :]
        model_cot[:rows, :] = term

    def finish(first, count):
        rows = count * ROWS
        here = pl.ds(first * ROWS, rows)
        g = grad[:rows, :]
        grad_gate = (g * factor_gate[here, :]).astype(jnp.bfloat16)
        grad_up = (g * factor_up[here, :]).astype(jnp.bfloat16)
        out_gate = dot(grad_gate, ph[...], (((1,), (0,)), ((), ())))
        out_up = dot(grad_up, ph[...], (((1,), (0,)), ((), ())))
        lane = lax.broadcasted_iota(jnp.int32, (rows, 2 * RANK), 1)
        right = jnp.concatenate(
            [
                jnp.where(lane < RANK, out_gate[:, : 2 * RANK], out_up[:, : 2 * RANK]),
                model_cot[:rows, 2 * RANK :],
            ],
            axis=1,
        )
        lead = block[first : first + count, :, D:].reshape(rows, 2 * RANK)
        left = jnp.concatenate(
            [lead.astype(jnp.float32), hidden_proj[here, 2 * RANK :]], axis=1
        )
        row = lax.broadcasted_iota(jnp.int32, (ROWS, 3 * RANK), 0)
        live = jnp.concatenate(
            [
                (row + owners[slot] * ROWS < live_count).astype(jnp.float32)
                for slot in range(first, first + count)
            ],
            axis=0,
        )
        total[...] += lax.dot_general(
            left * live,
            right,
            TN,
            precision=lax.Precision.HIGHEST,
            preferred_element_type=jnp.float32,
        )

    onward = {
        (1, DOWN): [(2, DOWN, slot_of(1, DOWN))],
        (2, DOWN): [(3, DOWN, slot_of(2, DOWN))],
        (3, DOWN): [(4, DOWN, slot_of(3, DOWN))],
        (1, UP): [(2, UP, slot_of(1, UP)), (2, ACROSS, slot_of(1, UP))],
        (2, UP): [(3, UP, slot_of(2, UP)), (3, ACROSS, slot_of(2, UP))],
        (3, ACROSS): [(4, UP, slot_of(3, ACROSS)), (4, ACROSS, slot_of(2, DOWN))],
        (4, UP): [(5, UP, slot_of(4, UP))],
        (4, ACROSS): [(5, DOWN, slot_of(4, ACROSS)), (5, ACROSS, slot_of(1, DOWN))],
    }
    for step in range(1, STEPS + 1):
        first, count = (0, 4) if step == 1 else (slot_of(step, 0), 3)
        for piece in range(PIECES):
            for link in (DOWN, UP, ACROSS):
                pass_on(step, link, piece).wait_recv()
                for later, way, slot in onward.get((step, link), ()):
                    send(later, way, piece, slot)
            if step == 1:
                load_weight[piece].wait()
            multiply(first, count, piece)
        finish(first, count)

    lane = lax.broadcasted_iota(jnp.int32, (RANK, 2 * RANK), 1)
    for k in range(3):
        rows = slice(k * RANK, (k + 1) * RANK)
        if k < 2:
            mine = total[rows, : 2 * RANK]
        else:
            mine = jnp.concatenate([total[rows, 2 * RANK :]] * 2, axis=1)
        swapped = pltpu.roll(mine, RANK, 1)
        turned[0, rows, :] = mine if k != 1 else swapped
        turned[1, rows, :] = swapped if k != 1 else mine
    lane = lax.broadcasted_iota(jnp.int32, (6, 2 * RANK), 1)
    for t in range(N):
        even = turned[0, pl.ds(12 * t, 6, stride=2), :]
        odd = turned[1, pl.ds(12 * t + 1, 6, stride=2), :]
        parts[t, :6, :] = jnp.where(lane < RANK, even, odd)

    def parts_copy(r):
        t = (me + r) % N
        return pltpu.make_async_remote_copy(
            src_ref=parts.at[t],
            dst_ref=parts_in.at[me],
            send_sem=parts_send.at[r],
            recv_sem=parts_recv.at[me],
            device_id=(dp, t),
            device_id_type=MESH,
        )

    def start_parts(r, carry):
        parts_copy(r).start()
        return carry

    lax.fori_loop(1, N, start_parts, 0)
    parts_in[me] = parts[me]

    def arrival(ref, sems, index):
        return pltpu.make_async_remote_copy(
            src_ref=ref.at[index],
            dst_ref=ref.at[index],
            send_sem=sems.at[index],
            recv_sem=sems.at[index],
            device_id=(dp, partner),
            device_id_type=MESH,
        )

    load_query.wait()

    def wait_query(r, carry):
        arrival(query_in, query_recv, (dp + r) % N).wait_recv()
        return carry

    lax.fori_loop(1, N, wait_query, 0)

    def wait_parts(r, carry):
        arrival(parts_in, parts_recv, (me + r) % N).wait_recv()
        return carry

    lax.fori_loop(1, N, wait_parts, 0)

    entries = jnp.sum(parts_in[...], axis=0)
    squares = jnp.sum(entries * entries)
    flat = jnp.concatenate([entries[i : i + 1, :] for i in range(6)], axis=1)
    high = flat.astype(jnp.bfloat16).astype(jnp.float32)
    row = lax.broadcasted_iota(jnp.int32, (16, SLICE), 0)
    pair = jnp.where(row == 0, high, jnp.where(row == 1, flat - high, 0.0))
    products = dot(pair.astype(jnp.bfloat16), query_in[...].reshape(N * 16, SLICE), NT)
    scores = products[0:1, :] + products[1:2, :]
    row = lax.broadcasted_iota(jnp.int32, (8, 128), 0)
    tile[...] = jnp.where(
        row == 0, scores[:, :128], jnp.where(row == 1, scores[:, 128:], squares)
    )

    def tile_copy(r):
        return pltpu.make_async_remote_copy(
            src_ref=tile,
            dst_ref=tiles_in.at[me],
            send_sem=tile_send.at[r],
            recv_sem=tile_recv.at[me],
            device_id=(dp, (me + r) % N),
            device_id_type=MESH,
        )

    def start_tile(r, carry):
        tile_copy(r).start()
        return carry

    lax.fori_loop(1, N, start_tile, 0)
    tiles_in[me] = tile[...]

    for copy in sent:
        copy.wait_send()

    def wait_sends(r, carry):
        query_copy(r).wait_send()
        parts_copy(r).wait_send()
        return carry

    lax.fori_loop(1, N, wait_sends, 0)

    def wait_tiles(r, carry):
        arrival(tiles_in, tile_recv, (me + r) % N).wait_recv()
        return carry

    lax.fori_loop(1, N, wait_tiles, 0)
    summed = jnp.sum(tiles_in[...], axis=0)
    norm = jnp.sqrt(summed[2:3, :] + 1e-06)
    out[:, :128] = summed[0:1, :] / norm
    out[:, 128:] = summed[1:2, :] / norm

    def wait_tile_sends(r, carry):
        tile_copy(r).wait_send()
        return carry

    lax.fori_loop(1, N, wait_tile_sends, 0)


def per_device(inputs, cotangent, gate_up, down_weight, proj_model, proj_hidden, lengths, queries):
    anywhere = pl.BlockSpec(memory_space=pl.ANY)
    bf16, f32 = jnp.bfloat16, jnp.float32
    dma = pltpu.SemaphoreType.DMA
    return pl.pallas_call(
        kernel,
        out_shape=jax.ShapeDtypeStruct((1, N * 16), f32),
        in_specs=[pl.BlockSpec(memory_space=pltpu.SMEM)] + [anywhere] * 7,
        out_specs=pl.BlockSpec(memory_space=pltpu.VMEM),
        scratch_shapes=[
            pltpu.VMEM((N, ROWS, WIDE), bf16),
            pltpu.VMEM((FF, D), bf16),
            pltpu.VMEM((2, N * ROWS, FF), bf16),
            pltpu.VMEM((N * ROWS, FF), f32),
            pltpu.VMEM((N * ROWS, FF), f32),
            pltpu.VMEM((ROWS, D), bf16),
            pltpu.VMEM((D, 3 * RANK), bf16),
            pltpu.VMEM((FF, 3 * RANK), bf16),
            pltpu.VMEM((N * ROWS, 3 * RANK), f32),
            pltpu.VMEM((4 * ROWS, FF), f32),
            pltpu.VMEM((4 * ROWS, 3 * RANK), f32),
            pltpu.VMEM((3 * RANK, 3 * RANK), f32),
            pltpu.VMEM((2, 3 * RANK, 2 * RANK), f32),
            pltpu.VMEM((N, 8, 128), f32),
            pltpu.VMEM((N, 8, 128), f32),
            pltpu.VMEM((N, 16, SLICE), bf16),
            pltpu.VMEM((8, 128), f32),
            pltpu.VMEM((N, 8, 128), f32),
            dma((5 + PIECES,)),
            dma((N,)),
            dma((3, STEPS, PIECES)),
            dma((3, STEPS, PIECES)),
            dma((N,)),
            dma((N,)),
            dma((N,)),
            dma((N,)),
            dma((N,)),
            dma((N,)),
        ],
        compiler_params=pltpu.CompilerParams(
            collective_id=0, has_side_effects=True, vmem_limit_bytes=48 * 1024 * 1024
        ),
        cost_estimate=pl.CostEstimate(
            flops=4 * 10**9, bytes_accessed=12 * 10**6, transcendentals=10**6
        ),
    )(lengths, inputs, cotangent, gate_up, down_weight, proj_model, proj_hidden, queries)


def solution(mesh):
    return jax.shard_map(
        per_device,
        mesh=mesh,
        in_specs=(
            P(("dp", "tensor"), None),
            P(("dp", "tensor"), None),
            P(None, "dp", "tensor"),
            P("tensor", None),
            P(),
            P("tensor", None),
            P("dp"),
            P("dp", None),
        ),
        out_specs=P("dp", None),
        check_vma=False,
    )
```

```python
import jax
import jax.numpy as jnp
from jax import lax
from jax.experimental import pallas as pl
from jax.experimental.pallas import tpu as pltpu
from jax.sharding import PartitionSpec as P

MESH = pl.DeviceIdType.MESH
RANK = 64
N = 16
STEPS = 5
PIECES = 2
D = 4096
FF = 896
ROWS = 32
WIDE = D + 2 * RANK
SLICE = 768
CUTS = tuple((D // PIECES * j, D // PIECES * (j + 1)) for j in range(PIECES))
NT = (((1,), (1,)), ((), ()))
OTHERS = [(4, 1), (4, 0)]
for far in (3, 2, 1):
    OTHERS += [(far, 1), (8 - far, 1), (far, 0), (8 - far, 0)]
OTHERS += [(0, 1)]

DOWN, UP, ACROSS = 0, 1, 2


def span(piece):
    low, high = CUTS[piece]
    return pl.ds(low, (WIDE if piece == PIECES - 1 else high) - low)


def slot_of(step, link):
    return 1 + 3 * (step - 1) + link


def dot(a, b, dims):
    return lax.dot_general(a, b, dims, preferred_element_type=jnp.float32)


def kernel(
    lengths,
    inputs,
    cotangent,
    gate_up,
    down_weight,
    proj_model,
    proj_hidden,
    queries,
    out,
    block,
    weight,
    gates,
    factor_up,
    factor_gate,
    x_rows,
    pm,
    ph,
    hidden_proj,
    grad,
    total,
    turned,
    parts,
    parts_in,
    query_in,
    tile,
    tiles_in,
    length,
    load_sem,
    gate_sem,
    send_sem,
    recv_sem,
    query_send,
    query_recv,
    parts_send,
    parts_recv,
    tile_send,
    tile_recv,
):
    dp = lax.axis_index("dp")
    me = lax.axis_index("tensor")
    z, b = me // 2, me % 2
    z_down, z_up = (z + 7) % 8, (z + 1) % 8
    partner = me + 1 - 2 * b
    target = {DOWN: z_up * 2 + b, UP: z_down * 2 + b, ACROSS: partner}

    y_hi, x, core = dp // 8, (dp // 2) % 4, dp % 2
    at = lambda y_hi, x, core: y_hi * 8 + x * 2 + core
    across = (at(1 - y_hi, x, core), partner)
    beside = (at(y_hi, x, 1 - core), me)
    x_up = (at(y_hi, (x + 1) % 4, core), me)
    x_down = (at(y_hi, (x + 3) % 4, core), me)

    owners = [me]
    same = lambda d: ((z + d + 8) % 8) * 2 + b
    opposite = lambda d: ((z + d + 8) % 8) * 2 + 1 - b
    for trio in (
        (same(-1), same(1), opposite(0)),
        (same(-2), same(2), opposite(1)),
        (same(-3), same(3), opposite(2)),
        (same(-4), opposite(3), opposite(-2)),
        (opposite(-3), opposite(4), opposite(-1)),
    ):
        owners += trio

    load_x = pltpu.make_async_copy(inputs, x_rows, load_sem.at[0])
    load_pm = pltpu.make_async_copy(proj_model.at[: 2 * RANK], pm, load_sem.at[1])
    load_last = pltpu.make_async_copy(
        proj_model.at[2 * RANK :], weight.at[FF:], load_sem.at[5 + PIECES]
    )
    load_own = pltpu.make_async_copy(cotangent, block.at[0, :, pl.ds(0, D)], load_sem.at[2])
    load_ph = pltpu.make_async_copy(proj_hidden, ph, load_sem.at[3])
    load_query = pltpu.make_async_copy(
        queries.at[:, pl.ds(pl.multiple_of(me * SLICE, 128), SLICE)],
        query_in.at[y_hi, x, core],
        load_sem.at[4],
    )
    load_weight = [
        pltpu.make_async_copy(
            down_weight.at[:, pl.ds(low, high - low)],
            weight.at[:FF, pl.ds(low, high - low)],
            load_sem.at[5 + j],
        )
        for j, (low, high) in enumerate(CUTS)
    ]
    load_gates = [
        pltpu.make_async_copy(
            gate_up.at[:, pl.ds(pl.multiple_of(owner * ROWS, ROWS), ROWS), :],
            gates.at[:, pl.ds(slot * ROWS, ROWS), :],
            gate_sem.at[slot],
        )
        for slot, owner in enumerate(owners)
    ]
    load_lengths = pltpu.make_async_copy(lengths, length, load_sem.at[6 + PIECES])
    load_lengths.start()
    load_x.start()
    load_pm.start()
    load_own.start()
    load_ph.start()
    for copy in load_gates:
        copy.start()
    load_last.start()
    for copy in load_weight:
        copy.start()
    load_query.start()

    barrier = pltpu.get_barrier_semaphore()

    for peer in [(dp, t) for t in target.values()] + [across, beside, x_up, x_down]:
        pl.semaphore_signal(barrier, inc=1, device_id=peer, device_id_type=MESH)
    pl.semaphore_wait(barrier, 7)

    def pass_on(step, link, piece, source=None):
        where = block.at[slot_of(step, link), :, span(piece)]
        return pltpu.make_async_remote_copy(
            src_ref=where if source is None else source,
            dst_ref=where,
            send_sem=send_sem.at[link, step - 1, piece],
            recv_sem=recv_sem.at[link, step - 1, piece],
            device_id=(dp, target[link]),
            device_id_type=MESH,
        )

    sent = []

    def send(step, link, piece, source_slot):
        copy = pass_on(step, link, piece, block.at[source_slot, :, span(piece)])
        copy.start()
        sent.append(copy)

    for link in (DOWN, UP, ACROSS):
        for piece in range(PIECES - 1):
            copy = pass_on(1, link, piece, cotangent.at[:, span(piece)])
            copy.start()
            sent.append(copy)

    load_x.wait()
    load_pm.wait()
    lead = dot(x_rows[...], pm[...], NT)
    load_own.wait()
    block[0, :, D:] = lead.astype(jnp.bfloat16)
    for link in (DOWN, UP, ACROSS):
        send(1, link, PIECES - 1, 0)

    def query_copy(source, slot, stage, peer):
        return pltpu.make_async_remote_copy(
            src_ref=source,
            dst_ref=query_in.at[slot],
            send_sem=query_send.at[stage],
            recv_sem=query_recv.at[stage],
            device_id=peer,
            device_id_type=MESH,
        )

    both = slice(None)
    x_before, x_after = (x + 3) % 4, (x + 1) % 4
    slots = [(y_hi, x, core), (both, x, core), (both, x), (both, x), (both, x_before)]
    arriving = [
        (1 - y_hi, x, core),
        (both, x, 1 - core),
        (both, x_before),
        (both, x_after),
        (both, (x + 2) % 4),
    ]
    peers = [across, beside, x_up, x_down, x_up]

    def send_queries(stage):
        if stage:
            source = query_in.at[slots[stage]]
        else:
            source = queries.at[:, pl.ds(pl.multiple_of(partner * SLICE, 128), SLICE)]
        copy = query_copy(source, slots[stage], stage, peers[stage])
        copy.start()
        sent.append(copy)

    def wait_queries(stage):
        here = query_in.at[arriving[stage]]
        query_copy(here, arriving[stage], stage, peers[stage]).wait_recv()

    send_queries(0)

    load_ph.wait()

    def gate_rows(i, carry):
        rows = pl.ds(pl.multiple_of(i * ROWS, ROWS), ROWS)
        g = gates[0, rows, :].astype(jnp.float32)
        u = gates[1, rows, :].astype(jnp.float32)
        s = jax.nn.sigmoid(g)
        silu = g * s
        factor_up[rows, :] = silu
        factor_gate[rows, :] = u * s * (1.0 + g * (1.0 - s))
        hidden = (silu * u).astype(jnp.bfloat16)
        hidden_proj[rows, :] = dot(hidden, ph[2 * RANK :, :], NT)
        return carry

    total[...] = jnp.zeros_like(total)
    parts[...] = jnp.zeros_like(parts)
    load_lengths.wait()
    live_count = length[0]

    def multiply(first, count, piece):
        low, high = CUTS[piece]
        rows = count * ROWS
        x = block[first : first + count, :, low:high].reshape(rows, high - low)
        for n in range(0, FF + RANK, 256):
            m = min(n + 256, FF + RANK)
            term = dot(x, weight[n:m, low:high], NT)
            if piece:
                term += grad[:rows, n:m]
            grad[:rows, n:m] = term

    def finish(first, count):
        rows = count * ROWS
        here = pl.ds(first * ROWS, rows)
        g = grad[:rows, :FF]
        grad_gate = (g * factor_gate[here, :]).astype(jnp.bfloat16)
        grad_up = (g * factor_up[here, :]).astype(jnp.bfloat16)
        lead = block[first : first + count, :, D:].reshape(rows, 2 * RANK)
        left = jnp.concatenate(
            [lead.astype(jnp.float32), hidden_proj[here, :]], axis=1
        )
        row = lax.broadcasted_iota(jnp.int32, (ROWS, 3 * RANK), 0)
        live = jnp.concatenate(
            [
                (row + owners[slot] * ROWS < live_count).astype(jnp.float32)
                for slot in range(first, first + count)
            ],
            axis=0,
        )
        left = (left * live).T
        rights = (
            dot(grad_gate, ph[:RANK, :], NT),
            dot(grad_up, ph[RANK : 2 * RANK, :], NT),
            grad[:rows, FF:],
        )
        for k, right in enumerate(rights):
            rows = slice(k * RANK, (k + 1) * RANK)
            total[rows, :] += jnp.dot(
                left[rows, :],
                right,
                precision=lax.Precision.HIGHEST,
                preferred_element_type=jnp.float32,
            )

    onward = {
        (1, DOWN): [(2, DOWN, slot_of(1, DOWN))],
        (2, DOWN): [(3, DOWN, slot_of(2, DOWN))],
        (3, DOWN): [(4, DOWN, slot_of(3, DOWN))],
        (1, UP): [(2, UP, slot_of(1, UP)), (2, ACROSS, slot_of(1, UP))],
        (2, UP): [(3, UP, slot_of(2, UP)), (3, ACROSS, slot_of(2, UP))],
        (3, ACROSS): [(4, UP, slot_of(3, ACROSS)), (4, ACROSS, slot_of(2, DOWN))],
        (4, UP): [(5, UP, slot_of(4, UP))],
        (4, ACROSS): [(5, DOWN, slot_of(4, ACROSS)), (5, ACROSS, slot_of(1, DOWN))],
    }
    for step in range(1, STEPS + 1):
        first, count = (0, 4) if step == 1 else (slot_of(step, 0), 3)
        for piece in range(PIECES):
            for link in (DOWN, UP, ACROSS):
                pass_on(step, link, piece).wait_recv()
                for later, way, slot in onward.get((step, link), ()):
                    send(later, way, piece, slot)
            if step == 1:
                if not piece:
                    load_last.wait()
                load_weight[piece].wait()
            multiply(first, count, piece)
            if not piece:
                for slot in range(first, first + count):
                    load_gates[slot].wait()
                lax.fori_loop(first, first + count, gate_rows, 0)
        if step == 1:
            load_query.wait()
            wait_queries(0)
            send_queries(1)
        if step == 2:
            wait_queries(1)
            send_queries(2)
            send_queries(3)
        if step == 3:
            wait_queries(2)
            send_queries(4)
        if step == 4:
            wait_queries(3)
            wait_queries(4)
        finish(first, count)

    turned[...] = jnp.concatenate([total[...], total[...]], axis=1)
    lane = lax.broadcasted_iota(jnp.int32, (6, 2 * RANK), 1)
    for t in range(N):
        even = turned[pl.ds(12 * t, 6, stride=2), :]
        odd = turned[pl.ds(12 * t + 1, 6, stride=2), :]
        parts[t, :6, :] = jnp.where(lane < RANK, even, odd)

    def other(r):
        far, over = OTHERS[r]
        return (z + far) % 8 * 2 + (1 - b if over else b)

    def exchange(source, target, sends, recvs):
        copies = []
        for r in range(N - 1):
            copy = pltpu.make_async_remote_copy(
                src_ref=source(other(r)),
                dst_ref=target(r),
                send_sem=sends.at[r],
                recv_sem=recvs.at[r],
                device_id=(dp, other(r)),
                device_id_type=MESH,
            )
            copy.start()
            copies.append(copy)
        return copies

    to_sum = exchange(
        lambda t: parts.at[t], lambda r: parts_in.at[r], parts_send, parts_recv
    )
    parts_in[N - 1] = parts[me]
    for copy in to_sum:
        copy.wait_recv()

    entries = jnp.sum(parts_in[...], axis=0)
    squares = jnp.sum(entries * entries)
    flat = jnp.concatenate([entries[i : i + 1, :] for i in range(6)], axis=1)
    high = flat.astype(jnp.bfloat16).astype(jnp.float32)
    row = lax.broadcasted_iota(jnp.int32, (16, SLICE), 0)
    pair = jnp.where(row == 0, high, jnp.where(row == 1, flat - high, 0.0))
    products = dot(pair.astype(jnp.bfloat16), query_in[...].reshape(N * 16, SLICE), NT)
    scores = products[0:1, :] + products[1:2, :]
    row = lax.broadcasted_iota(jnp.int32, (8, 128), 0)
    tile[...] = jnp.where(
        row == 0, scores[:, :128], jnp.where(row == 1, scores[:, 128:], squares)
    )

    to_add = exchange(
        lambda t: tile, lambda r: tiles_in.at[me], tile_send, tile_recv
    )
    tiles_in[me] = tile[...]
    for copy in sent + to_sum:
        copy.wait_send()
    for copy in to_add:
        copy.wait_recv()
    summed = jnp.sum(tiles_in[...], axis=0)
    norm = jnp.sqrt(summed[2:3, :] + 1e-06)
    out[:, :128] = summed[0:1, :] / norm
    out[:, 128:] = summed[1:2, :] / norm

    for copy in to_add:
        copy.wait_send()


def per_device(inputs, cotangent, gate_up, down_weight, proj_model, proj_hidden, lengths, queries):
    anywhere = pl.BlockSpec(memory_space=pl.ANY)
    bf16, f32 = jnp.bfloat16, jnp.float32
    dma = pltpu.SemaphoreType.DMA
    return pl.pallas_call(
        kernel,
        out_shape=jax.ShapeDtypeStruct((1, N * 16), f32),
        in_specs=[anywhere] * 8,
        out_specs=pl.BlockSpec(memory_space=pltpu.VMEM),
        scratch_shapes=[
            pltpu.VMEM((N, ROWS, WIDE), bf16),
            pltpu.VMEM((FF + RANK, D), bf16),
            pltpu.VMEM((2, N * ROWS, FF), bf16),
            pltpu.VMEM((N * ROWS, FF), f32),
            pltpu.VMEM((N * ROWS, FF), f32),
            pltpu.VMEM((ROWS, D), bf16),
            pltpu.VMEM((2 * RANK, D), bf16),
            pltpu.VMEM((3 * RANK, FF), bf16),
            pltpu.VMEM((N * ROWS, RANK), f32),
            pltpu.VMEM((4 * ROWS, FF + RANK), f32),
            pltpu.VMEM((3 * RANK, RANK), f32),
            pltpu.VMEM((3 * RANK, 2 * RANK), f32),
            pltpu.VMEM((N, 8, 128), f32),
            pltpu.VMEM((N, 8, 128), f32),
            pltpu.VMEM((2, 4, 2, 16, SLICE), bf16),
            pltpu.VMEM((8, 128), f32),
            pltpu.VMEM((N, 8, 128), f32),
            pltpu.SMEM((1,), jnp.int32),
            dma((7 + PIECES,)),
            dma((N,)),
            dma((3, STEPS, PIECES)),
            dma((3, STEPS, PIECES)),
            dma((5,)),
            dma((5,)),
            dma((N,)),
            dma((N,)),
            dma((N,)),
            dma((N,)),
        ],
        compiler_params=pltpu.CompilerParams(
            collective_id=0, has_side_effects=True, vmem_limit_bytes=54 * 1024 * 1024
        ),
        cost_estimate=pl.CostEstimate(
            flops=4 * 10**9, bytes_accessed=12 * 10**6, transcendentals=10**6
        ),
    )(lengths, inputs, cotangent, gate_up, down_weight, proj_model.T, proj_hidden.T, queries)


def solution(mesh):
    return jax.shard_map(
        per_device,
        mesh=mesh,
        in_specs=(
            P(("dp", "tensor"), None),
            P(("dp", "tensor"), None),
            P(None, "dp", "tensor"),
            P("tensor", None),
            P(),
            P("tensor", None),
            P("dp"),
            P("dp", None),
        ),
        out_specs=P("dp", None),
        check_vma=False,
    )
```

```python
import jax
import jax.numpy as jnp
from jax import lax
from jax.experimental import pallas as pl
from jax.experimental.pallas import tpu as pltpu
from jax.sharding import PartitionSpec as P

MESH = pl.DeviceIdType.MESH
RANK = 64
N = 16
STEPS = 5
PIECES = 3
D = 4096
FF = 896
ROWS = 32
WIDE = D + 2 * RANK
SLICE = 768
CUTS = ((0, 1408), (1408, 2816), (2816, D))
LEAD = CUTS[-1][0]
SHIFT = (0, 0, 2 * RANK)
NT = (((1,), (1,)), ((), ()))
OTHERS = [(4, 1), (4, 0)]
for far in (3, 2, 1):
    OTHERS += [(far, 1), (8 - far, 1), (far, 0), (8 - far, 0)]
OTHERS += [(0, 1)]

DOWN, UP, ACROSS = 0, 1, 2


def span(piece):
    low, high = CUTS[piece]
    if piece == PIECES - 2:
        high += 2 * RANK
    return pl.ds(low + SHIFT[piece], high - low)


def slot_of(step, link):
    return 1 + 3 * (step - 1) + link


def dot(a, b, dims):
    return lax.dot_general(a, b, dims, preferred_element_type=jnp.float32)


def kernel(
    lengths,
    inputs,
    cotangent,
    gate_up,
    down_weight,
    proj_model,
    proj_hidden,
    queries,
    out,
    block,
    weight,
    gates,
    factor_up,
    factor_gate,
    x_rows,
    pm,
    ph,
    hidden_proj,
    grad,
    sources,
    total,
    turned,
    parts,
    parts_in,
    query_in,
    tile,
    tiles_in,
    length,
    load_sem,
    gate_sem,
    send_sem,
    recv_sem,
    query_send,
    query_recv,
    parts_send,
    parts_recv,
    tile_send,
    tile_recv,
):
    dp = lax.axis_index("dp")
    me = lax.axis_index("tensor")
    z, b = me // 2, me % 2
    z_down, z_up = (z + 7) % 8, (z + 1) % 8
    partner = me + 1 - 2 * b
    target = {DOWN: z_up * 2 + b, UP: z_down * 2 + b, ACROSS: partner}

    y_hi, x, core = dp // 8, (dp // 2) % 4, dp % 2
    at = lambda y_hi, x, core: y_hi * 8 + x * 2 + core
    across = (at(1 - y_hi, x, core), partner)
    beside = (at(y_hi, x, 1 - core), me)
    x_up = (at(y_hi, (x + 1) % 4, core), me)
    x_down = (at(y_hi, (x + 3) % 4, core), me)

    owners = [me]
    same = lambda d: ((z + d + 8) % 8) * 2 + b
    opposite = lambda d: ((z + d + 8) % 8) * 2 + 1 - b
    for trio in (
        (same(-1), same(1), opposite(0)),
        (same(-2), same(2), opposite(1)),
        (same(-3), same(3), opposite(2)),
        (same(-4), opposite(3), opposite(-2)),
        (opposite(-3), opposite(4), opposite(-1)),
    ):
        owners += trio

    load_x = pltpu.make_async_copy(inputs, x_rows, load_sem.at[0])
    load_pm = pltpu.make_async_copy(proj_model.at[: 2 * RANK], pm, load_sem.at[1])
    load_last = pltpu.make_async_copy(
        proj_model.at[2 * RANK :], weight.at[FF:], load_sem.at[5 + PIECES]
    )
    load_own = [
        pltpu.make_async_copy(
            cotangent.at[:, pl.ds(low, high - low)],
            block.at[0, :, pl.ds(at, high - low)],
            load_sem.at[sem],
        )
        for low, high, at, sem in ((0, LEAD, 0, 2), (LEAD, D, LEAD + 2 * RANK, 7 + PIECES))
    ]
    load_ph = pltpu.make_async_copy(proj_hidden, ph, load_sem.at[3])
    load_query = pltpu.make_async_copy(
        queries.at[:, pl.ds(pl.multiple_of(me * SLICE, 128), SLICE)],
        query_in.at[y_hi, x, core],
        load_sem.at[4],
    )
    load_weight = [
        pltpu.make_async_copy(
            down_weight.at[:, pl.ds(low, high - low)],
            weight.at[:FF, pl.ds(low, high - low)],
            load_sem.at[5 + j],
        )
        for j, (low, high) in enumerate(CUTS)
    ]
    load_gates = [
        pltpu.make_async_copy(
            gate_up.at[:, pl.ds(pl.multiple_of(owner * ROWS, ROWS), ROWS), :],
            gates.at[:, pl.ds(slot * ROWS, ROWS), :],
            gate_sem.at[slot],
        )
        for slot, owner in enumerate(owners)
    ]
    load_lengths = pltpu.make_async_copy(lengths, length, load_sem.at[6 + PIECES])

    barrier = pltpu.get_barrier_semaphore()
    for peer in [(dp, t) for t in target.values()] + [across, beside, x_up, x_down]:
        pl.semaphore_signal(barrier, inc=1, device_id=peer, device_id_type=MESH)
    load_x.start()
    load_pm.start()
    for copy in load_own:
        copy.start()
    pl.semaphore_wait(barrier, 7)

    def pass_on(step, link, piece, source=None):
        where = block.at[slot_of(step, link), :, span(piece)]
        return pltpu.make_async_remote_copy(
            src_ref=where if source is None else source,
            dst_ref=where,
            send_sem=send_sem.at[link, step - 1, piece],
            recv_sem=recv_sem.at[link, step - 1, piece],
            device_id=(dp, target[link]),
            device_id_type=MESH,
        )

    sent = []

    def send(step, link, piece, source_slot):
        copy = pass_on(step, link, piece, block.at[source_slot, :, span(piece)])
        copy.start()
        sent.append(copy)

    first_sends = [
        pass_on(1, link, piece, cotangent.at[:, span(piece)])
        for piece in range(PIECES - 2)
        for link in (DOWN, UP, ACROSS)
    ]
    sent += first_sends

    def send_first(turn):
        @pl.when(core == turn)
        def _():
            for copy in first_sends:
                copy.start()

    send_first(0)
    load_ph.start()
    load_lengths.start()
    for copy in load_gates:
        copy.start()
    load_last.start()
    for copy in load_weight:
        copy.start()
    load_query.start()
    load_x.wait()
    send_first(1)
    load_pm.wait()
    lead = dot(x_rows[...], pm[...], NT)
    for copy in load_own:
        copy.wait()
    block[0, :, LEAD : LEAD + 2 * RANK] = lead.astype(jnp.bfloat16)
    for piece in (PIECES - 2, PIECES - 1):
        for link in (DOWN, UP, ACROSS):
            send(1, link, piece, 0)

    def query_copy(source, slot, stage, peer):
        return pltpu.make_async_remote_copy(
            src_ref=source,
            dst_ref=query_in.at[slot],
            send_sem=query_send.at[stage],
            recv_sem=query_recv.at[stage],
            device_id=peer,
            device_id_type=MESH,
        )

    both = slice(None)
    x_before, x_after = (x + 3) % 4, (x + 1) % 4
    slots = [(y_hi, x, core), (both, x, core), (both, x), (both, x), (both, x_before)]
    arriving = [
        (1 - y_hi, x, core),
        (both, x, 1 - core),
        (both, x_before),
        (both, x_after),
        (both, (x + 2) % 4),
    ]
    peers = [across, beside, x_up, x_down, x_up]

    def send_queries(stage):
        if stage:
            source = query_in.at[slots[stage]]
        else:
            source = queries.at[:, pl.ds(pl.multiple_of(partner * SLICE, 128), SLICE)]
        copy = query_copy(source, slots[stage], stage, peers[stage])
        copy.start()
        sent.append(copy)

    def wait_queries(stage):
        here = query_in.at[arriving[stage]]
        query_copy(here, arriving[stage], stage, peers[stage]).wait_recv()

    send_queries(0)

    load_ph.wait()

    def gate_rows(i, carry):
        rows = pl.ds(pl.multiple_of(i * ROWS, ROWS), ROWS)
        g = gates[0, rows, :].astype(jnp.float32)
        u = gates[1, rows, :].astype(jnp.float32)
        s = jax.nn.sigmoid(g)
        silu = g * s
        factor_up[rows, :] = silu
        factor_gate[rows, :] = u * s * (1.0 + g * (1.0 - s))
        hidden = (silu * u).astype(jnp.bfloat16)
        hidden_proj[rows, :] = dot(hidden, ph[2 * RANK :, :], NT)
        return carry

    total[...] = jnp.zeros_like(total)
    parts[...] = jnp.zeros_like(parts)
    load_lengths.wait()
    live_count = length[0]

    def multiply(first, count, piece):
        low, high = CUTS[piece]
        rows = count * ROWS
        at = low + SHIFT[piece]
        x = block[first : first + count, :, at : at + high - low].reshape(rows, high - low)
        for n in range(0, FF + RANK, 256):
            m = min(n + 256, FF + RANK)
            term = dot(x, weight[n:m, low:high], NT)
            if piece:
                term += grad[:rows, n:m]
            grad[:rows, n:m] = term

    def prepare(first, count):
        rows = count * ROWS
        here = pl.ds(first * ROWS, rows)
        lead = block[first : first + count, :, LEAD : LEAD + 2 * RANK].reshape(rows, 2 * RANK)
        row = lax.broadcasted_iota(jnp.int32, (ROWS, 3 * RANK), 0)
        live = jnp.concatenate(
            [
                (row + owners[slot] * ROWS < live_count).astype(jnp.float32)
                for slot in range(first, first + count)
            ],
            axis=0,
        )
        left = jnp.concatenate([lead.astype(jnp.float32), hidden_proj[here, :]], axis=1)
        sources[:, :rows] = (left * live).T

    def split(a):
        high = a.astype(jnp.bfloat16)
        return high, (a - high.astype(jnp.float32)).astype(jnp.bfloat16)

    def finish(first, count):
        rows = count * ROWS
        here = pl.ds(first * ROWS, rows)
        nn = (((1,), (0,)), ((), ()))
        source, source_low = split(sources[2 * RANK :, :rows])
        target, target_low = split(grad[:rows, FF:])
        last = dot(source, target, nn) + dot(source, target_low, nn)
        total[2 * RANK :, :] += last + dot(source_low, target, nn)
        for k, factor in enumerate((factor_gate, factor_up)):
            columns = slice(k * RANK, (k + 1) * RANK)
            moved = (grad[:rows, :FF] * factor[here, :]).astype(jnp.bfloat16)
            target, target_low = split(dot(moved, ph[columns, :], NT))
            source = sources[columns, :rows].astype(jnp.bfloat16)
            total[columns, :] += dot(source, target, nn) + dot(source, target_low, nn)

    onward = {
        (1, DOWN): [(2, DOWN, slot_of(1, DOWN))],
        (2, DOWN): [(3, DOWN, slot_of(2, DOWN))],
        (3, DOWN): [(4, DOWN, slot_of(3, DOWN))],
        (1, UP): [(2, UP, slot_of(1, UP)), (2, ACROSS, slot_of(1, UP))],
        (2, UP): [(3, UP, slot_of(2, UP)), (3, ACROSS, slot_of(2, UP))],
        (3, ACROSS): [(4, UP, slot_of(3, ACROSS)), (4, ACROSS, slot_of(2, DOWN))],
        (4, UP): [(5, UP, slot_of(4, UP))],
        (4, ACROSS): [(5, DOWN, slot_of(4, ACROSS)), (5, ACROSS, slot_of(1, DOWN))],
    }
    for step in range(1, STEPS + 1):
        first, count = (0, 4) if step == 1 else (slot_of(step, 0), 3)
        for piece in range(PIECES):
            for link in (DOWN, UP, ACROSS):
                pass_on(step, link, piece).wait_recv()
                for later, way, slot in onward.get((step, link), ()):
                    send(later, way, piece, slot)
            if step == 1:
                if not piece:
                    load_last.wait()
                load_weight[piece].wait()
            multiply(first, count, piece)
            if not piece:
                for slot in range(first, first + count):
                    load_gates[slot].wait()
                lax.fori_loop(first, first + count, gate_rows, 0)
            if piece == PIECES - 2:
                prepare(first, count)
        if step == 1:
            load_query.wait()
            wait_queries(0)
            send_queries(1)
        if step == 2:
            wait_queries(1)
            send_queries(2)
            send_queries(3)
        if step == 3:
            wait_queries(2)
            send_queries(4)
        if step == 4:
            wait_queries(3)
            wait_queries(4)
        finish(first, count)

    turned[...] = jnp.concatenate([total[...], total[...]], axis=1)
    lane = lax.broadcasted_iota(jnp.int32, (6, 2 * RANK), 1)
    for t in range(N):
        even = turned[pl.ds(12 * t, 6, stride=2), :]
        odd = turned[pl.ds(12 * t + 1, 6, stride=2), :]
        parts[t, :6, :] = jnp.where(lane < RANK, even, odd)

    def other(r):
        far, over = OTHERS[r]
        return (z + far) % 8 * 2 + (1 - b if over else b)

    def exchange(source, target, sends, recvs):
        copies = []
        for r in range(N - 1):
            copy = pltpu.make_async_remote_copy(
                src_ref=source(other(r)),
                dst_ref=target(r),
                send_sem=sends.at[r],
                recv_sem=recvs.at[r],
                device_id=(dp, other(r)),
                device_id_type=MESH,
            )
            copy.start()
            copies.append(copy)
        return copies

    to_sum = exchange(
        lambda t: parts.at[t], lambda r: parts_in.at[r], parts_send, parts_recv
    )
    parts_in[N - 1] = parts[me]
    for copy in to_sum:
        copy.wait_recv()

    entries = jnp.sum(parts_in[...], axis=0)
    squares = jnp.sum(entries * entries)
    flat = jnp.concatenate([entries[i : i + 1, :] for i in range(6)], axis=1)
    high = flat.astype(jnp.bfloat16).astype(jnp.float32)
    row = lax.broadcasted_iota(jnp.int32, (16, SLICE), 0)
    pair = jnp.where(row == 0, high, jnp.where(row == 1, flat - high, 0.0))
    products = dot(pair.astype(jnp.bfloat16), query_in[...].reshape(N * 16, SLICE), NT)
    scores = products[0:1, :] + products[1:2, :]
    row = lax.broadcasted_iota(jnp.int32, (8, 128), 0)
    tile[...] = jnp.where(
        row == 0, scores[:, :128], jnp.where(row == 1, scores[:, 128:], squares)
    )

    to_add = exchange(
        lambda t: tile, lambda r: tiles_in.at[me], tile_send, tile_recv
    )
    tiles_in[me] = tile[...]
    for copy in sent + to_sum:
        copy.wait_send()
    for copy in to_add:
        copy.wait_recv()
    summed = jnp.sum(tiles_in[...], axis=0)
    norm = jnp.sqrt(summed[2:3, :] + 1e-06)
    out[:, :128] = summed[0:1, :] / norm
    out[:, 128:] = summed[1:2, :] / norm

    for copy in to_add:
        copy.wait_send()


def per_device(inputs, cotangent, gate_up, down_weight, proj_model, proj_hidden, lengths, queries):
    anywhere = pl.BlockSpec(memory_space=pl.ANY)
    bf16, f32 = jnp.bfloat16, jnp.float32
    dma = pltpu.SemaphoreType.DMA
    return pl.pallas_call(
        kernel,
        out_shape=jax.ShapeDtypeStruct((1, N * 16), f32),
        in_specs=[anywhere] * 8,
        out_specs=pl.BlockSpec(memory_space=pltpu.VMEM),
        scratch_shapes=[
            pltpu.VMEM((N, ROWS, WIDE), bf16),
            pltpu.VMEM((FF + RANK, D), bf16),
            pltpu.VMEM((2, N * ROWS, FF), bf16),
            pltpu.VMEM((N * ROWS, FF), f32),
            pltpu.VMEM((N * ROWS, FF), f32),
            pltpu.VMEM((ROWS, D), bf16),
            pltpu.VMEM((2 * RANK, D), bf16),
            pltpu.VMEM((3 * RANK, FF), bf16),
            pltpu.VMEM((N * ROWS, RANK), f32),
            pltpu.VMEM((4 * ROWS, FF + RANK), f32),
            pltpu.VMEM((3 * RANK, 4 * ROWS), f32),
            pltpu.VMEM((3 * RANK, RANK), f32),
            pltpu.VMEM((3 * RANK, 2 * RANK), f32),
            pltpu.VMEM((N, 8, 128), f32),
            pltpu.VMEM((N, 8, 128), f32),
            pltpu.VMEM((2, 4, 2, 16, SLICE), bf16),
            pltpu.VMEM((8, 128), f32),
            pltpu.VMEM((N, 8, 128), f32),
            pltpu.SMEM((1,), jnp.int32),
            dma((8 + PIECES,)),
            dma((N,)),
            dma((3, STEPS, PIECES)),
            dma((3, STEPS, PIECES)),
            dma((5,)),
            dma((5,)),
            dma((N,)),
            dma((N,)),
            dma((N,)),
            dma((N,)),
        ],
        compiler_params=pltpu.CompilerParams(
            collective_id=0, has_side_effects=True, vmem_limit_bytes=55091 * 1024
        ),
        cost_estimate=pl.CostEstimate(
            flops=4 * 10**9, bytes_accessed=12 * 10**6, transcendentals=10**6
        ),
    )(lengths, inputs, cotangent, gate_up, down_weight, proj_model.T, proj_hidden.T, queries)


def solution(mesh):
    return jax.shard_map(
        per_device,
        mesh=mesh,
        in_specs=(
            P(("dp", "tensor"), None),
            P(("dp", "tensor"), None),
            P(None, "dp", "tensor"),
            P("tensor", None),
            P(),
            P("tensor", None),
            P("dp"),
            P("dp", None),
        ),
        out_specs=P("dp", None),
        check_vma=False,
    )
```

```python
import jax
import jax.numpy as jnp
from jax import lax
from jax.experimental import pallas as pl
from jax.experimental.pallas import tpu as pltpu
from jax.sharding import PartitionSpec as P

MESH = pl.DeviceIdType.MESH
RANK = 64
N = 16
STEPS = 5
PIECES = 3
D = 4096
FF = 896
ROWS = 32
WIDE = D + 2 * RANK
SLICES = 8
SLICE = 1536
LINES = SLICE // 128
CUTS = ((0, 1408), (1408, 2816), (2816, D))
LEAD = CUTS[-1][0]
SHIFT = (0, 0, 2 * RANK)
NT = (((1,), (1,)), ((), ()))
OTHERS = [(4, 1), (4, 0)]
for far in (3, 2, 1):
    OTHERS += [(far, 1), (8 - far, 1), (far, 0), (8 - far, 0)]
OTHERS += [(0, 1)]
NEAREST = [(2, 1), (2, 0), (7, 1), (1, 1), (7, 0), (1, 0), (0, 1)]

DOWN, UP, ACROSS = 0, 1, 2


def span(piece):
    low, high = CUTS[piece]
    if piece == PIECES - 2:
        high += 2 * RANK
    return pl.ds(low + SHIFT[piece], high - low)


def slot_of(step, link):
    return 1 + 3 * (step - 1) + link


def dot(a, b, dims):
    return lax.dot_general(a, b, dims, preferred_element_type=jnp.float32)


def kernel(
    lengths,
    inputs,
    cotangent,
    gate_up,
    down_weight,
    proj_model,
    proj_hidden,
    queries,
    out,
    block,
    weight,
    gates,
    factor_up,
    factor_gate,
    x_rows,
    pm,
    ph,
    hidden_proj,
    grad,
    sources,
    total,
    turned,
    parts,
    parts_in,
    query_in,
    tile,
    tiles_in,
    length,
    load_sem,
    gate_sem,
    send_sem,
    recv_sem,
    query_send,
    query_recv,
    parts_send,
    parts_recv,
    tile_send,
    tile_recv,
):
    dp = lax.axis_index("dp")
    me = lax.axis_index("tensor")
    z, b = me // 2, me % 2
    z_down, z_up = (z + 7) % 8, (z + 1) % 8
    partner = me + 1 - 2 * b
    slice_of = lambda z, b: z % 4 * 2 + b
    my_slice = slice_of(z, b)
    target = {DOWN: z_up * 2 + b, UP: z_down * 2 + b, ACROSS: partner}

    y_hi, x, core = dp // 8, (dp // 2) % 4, dp % 2
    at = lambda y_hi, x, core: y_hi * 8 + x * 2 + core
    across = (at(1 - y_hi, x, core), partner)
    beside = (at(y_hi, x, 1 - core), me)
    x_up = (at(y_hi, (x + 1) % 4, core), me)
    x_down = (at(y_hi, (x + 3) % 4, core), me)

    owners = [me]
    same = lambda d: ((z + d + 8) % 8) * 2 + b
    opposite = lambda d: ((z + d + 8) % 8) * 2 + 1 - b
    for trio in (
        (same(-1), same(1), opposite(0)),
        (same(-2), same(2), opposite(1)),
        (same(-3), same(3), opposite(2)),
        (same(-4), opposite(3), opposite(-2)),
        (opposite(-3), opposite(4), opposite(-1)),
    ):
        owners += trio

    load_x = pltpu.make_async_copy(inputs, x_rows, load_sem.at[0])
    load_pm = pltpu.make_async_copy(proj_model.at[: 2 * RANK], pm, load_sem.at[1])
    load_last = pltpu.make_async_copy(
        proj_model.at[2 * RANK :], weight.at[FF:], load_sem.at[5 + PIECES]
    )
    load_own = [
        pltpu.make_async_copy(
            cotangent.at[:, pl.ds(low, high - low)],
            block.at[0, :, pl.ds(at, high - low)],
            load_sem.at[sem],
        )
        for low, high, at, sem in ((0, LEAD, 0, 2), (LEAD, D, LEAD + 2 * RANK, 7 + PIECES))
    ]
    load_ph = pltpu.make_async_copy(proj_hidden, ph, load_sem.at[3])
    load_query = pltpu.make_async_copy(
        queries.at[:, pl.ds(pl.multiple_of(my_slice * SLICE, 128), SLICE)],
        query_in.at[y_hi, x, core],
        load_sem.at[4],
    )
    load_weight = [
        pltpu.make_async_copy(
            down_weight.at[:, pl.ds(low, high - low)],
            weight.at[:FF, pl.ds(low, high - low)],
            load_sem.at[5 + j],
        )
        for j, (low, high) in enumerate(CUTS)
    ]
    load_gates = [
        pltpu.make_async_copy(
            gate_up.at[:, pl.ds(pl.multiple_of(owner * ROWS, ROWS), ROWS), :],
            gates.at[:, pl.ds(slot * ROWS, ROWS), :],
            gate_sem.at[slot],
        )
        for slot, owner in enumerate(owners)
    ]
    load_lengths = pltpu.make_async_copy(lengths, length, load_sem.at[6 + PIECES])

    barrier = pltpu.get_barrier_semaphore()
    for peer in [(dp, t) for t in target.values()] + [across, beside, x_up, x_down]:
        pl.semaphore_signal(barrier, inc=1, device_id=peer, device_id_type=MESH)
    load_x.start()
    load_pm.start()
    for copy in load_own:
        copy.start()
    pl.semaphore_wait(barrier, 7)

    def pass_on(step, link, piece, source=None):
        where = block.at[slot_of(step, link), :, span(piece)]
        return pltpu.make_async_remote_copy(
            src_ref=where if source is None else source,
            dst_ref=where,
            send_sem=send_sem.at[link, step - 1, piece],
            recv_sem=recv_sem.at[link, step - 1, piece],
            device_id=(dp, target[link]),
            device_id_type=MESH,
        )

    sent = []

    def send(step, link, piece, source_slot):
        copy = pass_on(step, link, piece, block.at[source_slot, :, span(piece)])
        copy.start()
        sent.append(copy)

    first_sends = [
        pass_on(1, link, piece, cotangent.at[:, span(piece)])
        for piece in range(PIECES - 2)
        for link in (DOWN, UP, ACROSS)
    ]
    sent += first_sends

    def send_first(turn):
        @pl.when(core == turn)
        def _():
            for copy in first_sends:
                copy.start()

    send_first(0)
    load_ph.start()
    load_lengths.start()
    for copy in load_gates:
        copy.start()
    load_last.start()
    for copy in load_weight:
        copy.start()
    load_query.start()
    load_x.wait()
    send_first(1)
    load_pm.wait()
    lead = dot(x_rows[...], pm[...], NT)
    for copy in load_own:
        copy.wait()
    block[0, :, LEAD : LEAD + 2 * RANK] = lead.astype(jnp.bfloat16)
    for piece in (PIECES - 2, PIECES - 1):
        for link in (DOWN, UP, ACROSS):
            send(1, link, piece, 0)

    def query_copy(source, slot, stage, peer):
        return pltpu.make_async_remote_copy(
            src_ref=source,
            dst_ref=query_in.at[slot],
            send_sem=query_send.at[stage],
            recv_sem=query_recv.at[stage],
            device_id=peer,
            device_id_type=MESH,
        )

    both = slice(None)
    x_before, x_after = (x + 3) % 4, (x + 1) % 4
    slots = [(y_hi, x, core), (both, x, core), (both, x), (both, x), (both, x_before)]
    arriving = [
        (1 - y_hi, x, core),
        (both, x, 1 - core),
        (both, x_before),
        (both, x_after),
        (both, (x + 2) % 4),
    ]
    peers = [across, beside, x_up, x_down, x_up]

    def send_queries(stage):
        if stage:
            source = query_in.at[slots[stage]]
        else:
            begin = pl.multiple_of(slice_of(z, 1 - b) * SLICE, 128)
            source = queries.at[:, pl.ds(begin, SLICE)]
        copy = query_copy(source, slots[stage], stage, peers[stage])
        copy.start()
        sent.append(copy)

    def wait_queries(stage):
        here = query_in.at[arriving[stage]]
        query_copy(here, arriving[stage], stage, peers[stage]).wait_recv()

    send_queries(0)

    load_ph.wait()

    def gate_rows(i, carry):
        rows = pl.ds(pl.multiple_of(i * ROWS, ROWS), ROWS)
        g = gates[0, rows, :].astype(jnp.float32)
        u = gates[1, rows, :].astype(jnp.float32)
        s = jax.nn.sigmoid(g)
        silu = g * s
        factor_up[rows, :] = silu
        factor_gate[rows, :] = u * s * (1.0 + g * (1.0 - s))
        hidden = (silu * u).astype(jnp.bfloat16)
        hidden_proj[rows, :] = dot(hidden, ph[2 * RANK :, :], NT)
        return carry

    total[...] = jnp.zeros_like(total)
    parts[...] = jnp.zeros_like(parts)
    load_lengths.wait()
    live_count = length[0]

    def multiply(first, count, piece):
        low, high = CUTS[piece]
        rows = count * ROWS
        at = low + SHIFT[piece]
        x = block[first : first + count, :, at : at + high - low].reshape(rows, high - low)
        for n in range(0, FF + RANK, 256):
            m = min(n + 256, FF + RANK)
            term = dot(x, weight[n:m, low:high], NT)
            if piece:
                term += grad[:rows, n:m]
            grad[:rows, n:m] = term

    def prepare(first, count):
        rows = count * ROWS
        here = pl.ds(first * ROWS, rows)
        lead = block[first : first + count, :, LEAD : LEAD + 2 * RANK].reshape(rows, 2 * RANK)
        row = lax.broadcasted_iota(jnp.int32, (ROWS, 3 * RANK), 0)
        live = jnp.concatenate(
            [
                (row + owners[slot] * ROWS < live_count).astype(jnp.float32)
                for slot in range(first, first + count)
            ],
            axis=0,
        )
        left = jnp.concatenate([lead.astype(jnp.float32), hidden_proj[here, :]], axis=1)
        sources[:, :rows] = (left * live).T

    def split(a):
        high = a.astype(jnp.bfloat16)
        return high, (a - high.astype(jnp.float32)).astype(jnp.bfloat16)

    def finish(first, count):
        rows = count * ROWS
        here = pl.ds(first * ROWS, rows)
        nn = (((1,), (0,)), ((), ()))
        source, source_low = split(sources[2 * RANK :, :rows])
        target, target_low = split(grad[:rows, FF:])
        last = dot(source, target, nn) + dot(source, target_low, nn)
        total[2 * RANK :, :] += last + dot(source_low, target, nn)
        for k, factor in enumerate((factor_gate, factor_up)):
            columns = slice(k * RANK, (k + 1) * RANK)
            moved = (grad[:rows, :FF] * factor[here, :]).astype(jnp.bfloat16)
            target, target_low = split(dot(moved, ph[columns, :], NT))
            source = sources[columns, :rows].astype(jnp.bfloat16)
            total[columns, :] += dot(source, target, nn) + dot(source, target_low, nn)

    onward = {
        (1, DOWN): [(2, DOWN, slot_of(1, DOWN))],
        (2, DOWN): [(3, DOWN, slot_of(2, DOWN))],
        (3, DOWN): [(4, DOWN, slot_of(3, DOWN))],
        (1, UP): [(2, UP, slot_of(1, UP)), (2, ACROSS, slot_of(1, UP))],
        (2, UP): [(3, UP, slot_of(2, UP)), (3, ACROSS, slot_of(2, UP))],
        (3, ACROSS): [(4, UP, slot_of(3, ACROSS)), (4, ACROSS, slot_of(2, DOWN))],
        (4, UP): [(5, UP, slot_of(4, UP))],
        (4, ACROSS): [(5, DOWN, slot_of(4, ACROSS)), (5, ACROSS, slot_of(1, DOWN))],
    }
    for step in range(1, STEPS + 1):
        first, count = (0, 4) if step == 1 else (slot_of(step, 0), 3)
        for piece in range(PIECES):
            for link in (DOWN, UP, ACROSS):
                pass_on(step, link, piece).wait_recv()
                for later, way, slot in onward.get((step, link), ()):
                    send(later, way, piece, slot)
            if step == 1:
                if not piece:
                    load_last.wait()
                load_weight[piece].wait()
            multiply(first, count, piece)
            if not piece:
                for slot in range(first, first + count):
                    load_gates[slot].wait()
                lax.fori_loop(first, first + count, gate_rows, 0)
            if piece == PIECES - 2:
                prepare(first, count)
        if step == 1:
            load_query.wait()
            wait_queries(0)
            send_queries(1)
        if step == 2:
            wait_queries(1)
            send_queries(2)
            send_queries(3)
        if step == 3:
            wait_queries(2)
            send_queries(4)
        if step == 4:
            wait_queries(3)
            wait_queries(4)
        finish(first, count)

    turned[...] = jnp.concatenate([total[...], total[...]], axis=1)
    lane = lax.broadcasted_iota(jnp.int32, (LINES, 2 * RANK), 1)
    for i in range(SLICES):
        even = turned[pl.ds(2 * LINES * i, LINES, stride=2), :]
        odd = turned[pl.ds(2 * LINES * i + 1, LINES, stride=2), :]
        parts[i, :LINES, :] = jnp.where(lane < RANK, even, odd)

    def exchange(ways, peer_of, source, target, sends, recvs):
        copies = []
        for r, (far, over) in enumerate(ways):
            peer = (peer_of(far), 1 - b if over else b)
            copy = pltpu.make_async_remote_copy(
                src_ref=source(*peer),
                dst_ref=target,
                send_sem=sends.at[r],
                recv_sem=recvs.at[r],
                device_id=(dp, peer[0] * 2 + peer[1]),
                device_id_type=MESH,
            )
            copy.start()
            copies.append(copy)
        return copies

    to_sum = exchange(
        OTHERS,
        lambda far: (z + far) % 8,
        lambda z, b: parts.at[slice_of(z, b)],
        parts_in.at[me],
        parts_send,
        parts_recv,
    )
    parts_in[me] = parts[my_slice]
    for copy in to_sum:
        copy.wait_recv()

    entries = jnp.sum(parts_in[...], axis=0)
    squares = jnp.sum(entries * entries)
    flat = jnp.concatenate([entries[i : i + 1, :] for i in range(LINES)], axis=1)
    high = flat.astype(jnp.bfloat16).astype(jnp.float32)
    row = lax.broadcasted_iota(jnp.int32, (16, SLICE), 0)
    pair = jnp.where(row == 0, high, jnp.where(row == 1, flat - high, 0.0))
    products = dot(pair.astype(jnp.bfloat16), query_in[...].reshape(N * 16, SLICE), NT)
    scores = products[0:1, :] + products[1:2, :]
    row = lax.broadcasted_iota(jnp.int32, (8, 128), 0)
    tile[...] = jnp.where(
        row == 0, scores[:, :128], jnp.where(row == 1, scores[:, 128:], squares)
    )

    to_add = exchange(
        NEAREST,
        lambda far: (z + 8 - far) % 8,
        lambda z, b: tile,
        tiles_in.at[my_slice],
        tile_send,
        tile_recv,
    )
    tiles_in[my_slice] = tile[...]
    for copy in sent + to_sum:
        copy.wait_send()
    for copy in to_add:
        copy.wait_recv()
    summed = jnp.sum(tiles_in[...], axis=0)
    norm = jnp.sqrt(summed[2:3, :] + 1e-06)
    out[:, :128] = summed[0:1, :] / norm
    out[:, 128:] = summed[1:2, :] / norm

    for copy in to_add:
        copy.wait_send()


def per_device(inputs, cotangent, gate_up, down_weight, proj_model, proj_hidden, lengths, queries):
    anywhere = pl.BlockSpec(memory_space=pl.ANY)
    bf16, f32 = jnp.bfloat16, jnp.float32
    dma = pltpu.SemaphoreType.DMA
    return pl.pallas_call(
        kernel,
        out_shape=jax.ShapeDtypeStruct((1, N * 16), f32),
        in_specs=[anywhere] * 8,
        out_specs=pl.BlockSpec(memory_space=pltpu.VMEM),
        scratch_shapes=[
            pltpu.VMEM((N, ROWS, WIDE), bf16),
            pltpu.VMEM((FF + RANK, D), bf16),
            pltpu.VMEM((2, N * ROWS, FF), bf16),
            pltpu.VMEM((N * ROWS, FF), f32),
            pltpu.VMEM((N * ROWS, FF), f32),
            pltpu.VMEM((ROWS, D), bf16),
            pltpu.VMEM((2 * RANK, D), bf16),
            pltpu.VMEM((3 * RANK, FF), bf16),
            pltpu.VMEM((N * ROWS, RANK), f32),
            pltpu.VMEM((4 * ROWS, FF + RANK), f32),
            pltpu.VMEM((3 * RANK, 4 * ROWS), f32),
            pltpu.VMEM((3 * RANK, RANK), f32),
            pltpu.VMEM((3 * RANK, 2 * RANK), f32),
            pltpu.VMEM((SLICES, 16, 128), f32),
            pltpu.VMEM((N, 16, 128), f32),
            pltpu.VMEM((2, 4, 2, 16, SLICE), bf16),
            pltpu.VMEM((8, 128), f32),
            pltpu.VMEM((SLICES, 8, 128), f32),
            pltpu.SMEM((1,), jnp.int32),
            dma((8 + PIECES,)),
            dma((N,)),
            dma((3, STEPS, PIECES)),
            dma((3, STEPS, PIECES)),
            dma((5,)),
            dma((5,)),
            dma((N,)),
            dma((N,)),
            dma((N,)),
            dma((N,)),
        ],
        compiler_params=pltpu.CompilerParams(
            collective_id=0, has_side_effects=True, vmem_limit_bytes=55091 * 1024
        ),
        cost_estimate=pl.CostEstimate(
            flops=4 * 10**9, bytes_accessed=12 * 10**6, transcendentals=10**6
        ),
    )(lengths, inputs, cotangent, gate_up, down_weight, proj_model.T, proj_hidden.T, queries)


def solution(mesh):
    return jax.shard_map(
        per_device,
        mesh=mesh,
        in_specs=(
            P(("dp", "tensor"), None),
            P(("dp", "tensor"), None),
            P(None, "dp", "tensor"),
            P("tensor", None),
            P(),
            P("tensor", None),
            P("dp"),
            P("dp", None),
        ),
        out_specs=P("dp", None),
        check_vma=False,
    )
```

```python
import jax
import jax.numpy as jnp
from jax import lax
from jax.experimental import pallas as pl
from jax.experimental.pallas import tpu as pltpu
from jax.sharding import PartitionSpec as P

MESH = pl.DeviceIdType.MESH
RANK = 64
N = 16
STEPS = 5
PIECES = 3
D = 4096
FF = 896
ROWS = 32
WIDE = D + 2 * RANK
SLICES = 8
SLICE = 1536
LINES = SLICE // 128
CUTS = ((0, 1408), (1408, 2816), (2816, D))
LEAD = CUTS[-1][0]
SHIFT = (0, 0, 2 * RANK)
NT = (((1,), (1,)), ((), ()))
OTHERS = [(4, 1), (4, 0)]
for far in (3, 2, 1):
    OTHERS += [(far, 1), (8 - far, 1), (far, 0), (8 - far, 0)]
OTHERS += [(0, 1)]
NEAREST = [(2, 1), (2, 0), (7, 1), (1, 1), (7, 0), (1, 0), (0, 1)]

DOWN, UP, ACROSS = 0, 1, 2


def span(piece):
    low, high = CUTS[piece]
    if piece == PIECES - 2:
        high += 2 * RANK
    return pl.ds(low + SHIFT[piece], high - low)


def slot_of(step, link):
    return 1 + 3 * (step - 1) + link


def dot(a, b, dims):
    return lax.dot_general(a, b, dims, preferred_element_type=jnp.float32)


def kernel(
    lengths,
    inputs,
    cotangent,
    gate_up,
    down_weight,
    proj_model,
    proj_hidden,
    queries,
    out,
    block,
    weight,
    gates,
    factor_up,
    factor_gate,
    x_rows,
    pm,
    ph,
    hidden_proj,
    grad,
    sources,
    total,
    turned,
    parts,
    parts_in,
    query_in,
    tile,
    tiles_in,
    length,
    load_sem,
    gate_sem,
    send_sem,
    recv_sem,
    query_send,
    query_recv,
    parts_send,
    parts_recv,
    tile_send,
    tile_recv,
):
    dp = lax.axis_index("dp")
    me = lax.axis_index("tensor")
    z, b = me // 2, me % 2
    z_down, z_up = (z + 7) % 8, (z + 1) % 8
    partner = me + 1 - 2 * b
    slice_of = lambda z, b: z % 4 * 2 + b
    my_slice = slice_of(z, b)
    target = {DOWN: z_up * 2 + b, UP: z_down * 2 + b, ACROSS: partner}

    y_hi, x, core = dp // 8, (dp // 2) % 4, dp % 2
    at = lambda y_hi, x, core: y_hi * 8 + x * 2 + core
    across = (at(1 - y_hi, x, core), partner)
    beside = (at(y_hi, x, 1 - core), me)
    x_up = (at(y_hi, (x + 1) % 4, core), me)
    x_down = (at(y_hi, (x + 3) % 4, core), me)

    owners = [me]
    same = lambda d: ((z + d + 8) % 8) * 2 + b
    opposite = lambda d: ((z + d + 8) % 8) * 2 + 1 - b
    for trio in (
        (same(-1), same(1), opposite(0)),
        (same(-2), same(2), opposite(1)),
        (same(-3), same(3), opposite(2)),
        (same(-4), opposite(3), opposite(-2)),
        (opposite(-3), opposite(4), opposite(-1)),
    ):
        owners += trio

    load_x = pltpu.make_async_copy(inputs, x_rows, load_sem.at[0])
    load_pm = pltpu.make_async_copy(proj_model.at[: 2 * RANK], pm, load_sem.at[1])
    load_last = pltpu.make_async_copy(
        proj_model.at[2 * RANK :], weight.at[FF:], load_sem.at[5 + PIECES]
    )
    load_own = [
        pltpu.make_async_copy(
            cotangent.at[:, pl.ds(low, high - low)],
            block.at[0, :, pl.ds(at, high - low)],
            load_sem.at[sem],
        )
        for low, high, at, sem in ((0, LEAD, 0, 2), (LEAD, D, LEAD + 2 * RANK, 7 + PIECES))
    ]
    load_ph = pltpu.make_async_copy(proj_hidden, ph, load_sem.at[3])
    load_query = pltpu.make_async_copy(
        queries.at[:, pl.ds(pl.multiple_of(my_slice * SLICE, 128), SLICE)],
        query_in.at[y_hi, x, core],
        load_sem.at[4],
    )
    load_weight = [
        pltpu.make_async_copy(
            down_weight.at[:, pl.ds(low, high - low)],
            weight.at[:FF, pl.ds(low, high - low)],
            load_sem.at[5 + j],
        )
        for j, (low, high) in enumerate(CUTS)
    ]
    load_gates = [
        pltpu.make_async_copy(
            gate_up.at[:, pl.ds(pl.multiple_of(owner * ROWS, ROWS), ROWS), :],
            gates.at[:, pl.ds(slot * ROWS, ROWS), :],
            gate_sem.at[slot],
        )
        for slot, owner in enumerate(owners)
    ]
    load_lengths = pltpu.make_async_copy(lengths, length, load_sem.at[6 + PIECES])

    barrier = pltpu.get_barrier_semaphore()
    for peer in [(dp, t) for t in target.values()] + [across, beside, x_up, x_down]:
        pl.semaphore_signal(barrier, inc=1, device_id=peer, device_id_type=MESH)
    load_x.start()
    load_pm.start()
    for copy in load_own:
        copy.start()
    pl.semaphore_wait(barrier, 7)

    def pass_on(step, link, piece, source=None):
        where = block.at[slot_of(step, link), :, span(piece)]
        return pltpu.make_async_remote_copy(
            src_ref=where if source is None else source,
            dst_ref=where,
            send_sem=send_sem.at[link, step - 1, piece],
            recv_sem=recv_sem.at[link, step - 1, piece],
            device_id=(dp, target[link]),
            device_id_type=MESH,
        )

    sent = []

    def send(step, link, piece, source_slot):
        copy = pass_on(step, link, piece, block.at[source_slot, :, span(piece)])
        copy.start()
        sent.append(copy)

    first_sends = [
        pass_on(1, link, piece, cotangent.at[:, span(piece)])
        for piece in range(PIECES - 2)
        for link in (DOWN, UP, ACROSS)
    ]
    sent += first_sends

    def send_first(turn):
        @pl.when(core == turn)
        def _():
            for copy in first_sends:
                copy.start()

    send_first(0)
    load_ph.start()
    load_lengths.start()
    for copy in load_gates:
        copy.start()
    load_last.start()
    for copy in load_weight:
        copy.start()
    load_query.start()
    load_x.wait()
    send_first(1)
    load_pm.wait()
    lead = dot(x_rows[...], pm[...], NT)
    for copy in load_own:
        copy.wait()
    block[0, :, LEAD : LEAD + 2 * RANK] = lead.astype(jnp.bfloat16)
    for piece in (PIECES - 2, PIECES - 1):
        for link in (DOWN, UP, ACROSS):
            send(1, link, piece, 0)

    def query_copy(source, slot, stage, peer):
        return pltpu.make_async_remote_copy(
            src_ref=source,
            dst_ref=query_in.at[slot],
            send_sem=query_send.at[stage],
            recv_sem=query_recv.at[stage],
            device_id=peer,
            device_id_type=MESH,
        )

    both = slice(None)
    x_before, x_after = (x + 3) % 4, (x + 1) % 4
    slots = [(y_hi, x, core), (both, x, core), (both, x), (both, x), (both, x_before)]
    arriving = [
        (1 - y_hi, x, core),
        (both, x, 1 - core),
        (both, x_before),
        (both, x_after),
        (both, (x + 2) % 4),
    ]
    peers = [across, beside, x_up, x_down, x_up]

    def send_queries(stage):
        if stage:
            source = query_in.at[slots[stage]]
        else:
            begin = pl.multiple_of(slice_of(z, 1 - b) * SLICE, 128)
            source = queries.at[:, pl.ds(begin, SLICE)]
        copy = query_copy(source, slots[stage], stage, peers[stage])
        copy.start()
        sent.append(copy)

    def wait_queries(stage):
        here = query_in.at[arriving[stage]]
        query_copy(here, arriving[stage], stage, peers[stage]).wait_recv()

    send_queries(0)

    load_ph.wait()

    def gate_rows(i, carry):
        rows = pl.ds(pl.multiple_of(i * ROWS, ROWS), ROWS)
        g = gates[0, rows, :].astype(jnp.float32)
        u = gates[1, rows, :].astype(jnp.float32)
        s = jax.nn.sigmoid(g)
        silu = g * s
        factor_up[rows, :] = silu
        factor_gate[rows, :] = u * s * (1.0 + g * (1.0 - s))
        hidden = (silu * u).astype(jnp.bfloat16)
        hidden_proj[rows, :] = dot(hidden, ph[2 * RANK :, :], NT)
        return carry

    total[...] = jnp.zeros_like(total)
    parts[...] = jnp.zeros_like(parts)
    load_lengths.wait()
    live_count = length[0]

    def multiply(first, count, piece):
        low, high = CUTS[piece]
        rows = count * ROWS
        at = low + SHIFT[piece]
        x = block[first : first + count, :, at : at + high - low].reshape(rows, high - low)
        for n in range(0, FF + RANK, 256):
            m = min(n + 256, FF + RANK)
            term = dot(x, weight[n:m, low:high], NT)
            if piece:
                term += grad[:rows, n:m]
            grad[:rows, n:m] = term

    def prepare(first, count):
        rows = count * ROWS
        here = pl.ds(first * ROWS, rows)
        lead = block[first : first + count, :, LEAD : LEAD + 2 * RANK].reshape(rows, 2 * RANK)
        row = lax.broadcasted_iota(jnp.int32, (ROWS, 3 * RANK), 0)
        live = jnp.concatenate(
            [
                (row + owners[slot] * ROWS < live_count).astype(jnp.float32)
                for slot in range(first, first + count)
            ],
            axis=0,
        )
        left = jnp.concatenate([lead.astype(jnp.float32), hidden_proj[here, :]], axis=1)
        sources[:, :rows] = (left * live).T

    def split(a):
        high = a.astype(jnp.bfloat16)
        return high, (a - high.astype(jnp.float32)).astype(jnp.bfloat16)

    def finish(first, count):
        rows = count * ROWS
        here = pl.ds(first * ROWS, rows)
        nn = (((1,), (0,)), ((), ()))
        source, source_low = split(sources[2 * RANK :, :rows])
        target, target_low = split(grad[:rows, FF:])
        last = dot(source, target, nn) + dot(source, target_low, nn)
        total[2 * RANK :, :] += last + dot(source_low, target, nn)
        for k, factor in enumerate((factor_gate, factor_up)):
            columns = slice(k * RANK, (k + 1) * RANK)
            moved = (grad[:rows, :FF] * factor[here, :]).astype(jnp.bfloat16)
            target, target_low = split(dot(moved, ph[columns, :], NT))
            source = sources[columns, :rows].astype(jnp.bfloat16)
            total[columns, :] += dot(source, target, nn) + dot(source, target_low, nn)

    onward = {
        (1, DOWN): [(2, DOWN, slot_of(1, DOWN))],
        (2, DOWN): [(3, DOWN, slot_of(2, DOWN))],
        (3, DOWN): [(4, DOWN, slot_of(3, DOWN))],
        (1, UP): [(2, UP, slot_of(1, UP)), (2, ACROSS, slot_of(1, UP))],
        (2, UP): [(3, UP, slot_of(2, UP)), (3, ACROSS, slot_of(2, UP))],
        (3, ACROSS): [(4, UP, slot_of(3, ACROSS)), (4, ACROSS, slot_of(2, DOWN))],
        (4, UP): [(5, UP, slot_of(4, UP))],
        (4, ACROSS): [(5, DOWN, slot_of(4, ACROSS)), (5, ACROSS, slot_of(1, DOWN))],
    }
    for step in range(1, STEPS + 1):
        first, count = (0, 4) if step == 1 else (slot_of(step, 0), 3)
        for piece in range(PIECES):
            for link in (ACROSS, UP, DOWN):
                pass_on(step, link, piece).wait_recv()
                for later, way, slot in onward.get((step, link), ()):
                    send(later, way, piece, slot)
            if step == 1:
                if not piece:
                    load_last.wait()
                load_weight[piece].wait()
            multiply(first, count, piece)
            if not piece:
                for slot in range(first, first + count):
                    load_gates[slot].wait()
                lax.fori_loop(first, first + count, gate_rows, 0)
            if piece == PIECES - 2:
                prepare(first, count)
        if step == 1:
            load_query.wait()
            wait_queries(0)
            send_queries(1)
        if step == 2:
            wait_queries(1)
            send_queries(2)
            send_queries(3)
        if step == 3:
            wait_queries(2)
            send_queries(4)
        if step == 4:
            wait_queries(3)
            wait_queries(4)
        finish(first, count)

    turned[...] = jnp.concatenate([total[...], total[...]], axis=1)
    lane = lax.broadcasted_iota(jnp.int32, (LINES, 2 * RANK), 1)
    for i in range(SLICES):
        even = turned[pl.ds(2 * LINES * i, LINES, stride=2), :]
        odd = turned[pl.ds(2 * LINES * i + 1, LINES, stride=2), :]
        parts[i, :LINES, :] = jnp.where(lane < RANK, even, odd)

    def exchange(ways, peer_of, source, target, sends, recvs):
        copies = []
        for r, (far, over) in enumerate(ways):
            peer = (peer_of(far), 1 - b if over else b)
            copy = pltpu.make_async_remote_copy(
                src_ref=source(*peer),
                dst_ref=target,
                send_sem=sends.at[r],
                recv_sem=recvs.at[r],
                device_id=(dp, peer[0] * 2 + peer[1]),
                device_id_type=MESH,
            )
            copy.start()
            copies.append(copy)
        return copies

    to_sum = exchange(
        OTHERS,
        lambda far: (z + far) % 8,
        lambda z, b: parts.at[slice_of(z, b)],
        parts_in.at[me],
        parts_send,
        parts_recv,
    )
    parts_in[me] = parts[my_slice]
    for copy in to_sum:
        copy.wait_recv()

    entries = jnp.sum(parts_in[...], axis=0)
    squares = jnp.sum(entries * entries)
    flat = jnp.concatenate([entries[i : i + 1, :] for i in range(LINES)], axis=1)
    high = flat.astype(jnp.bfloat16).astype(jnp.float32)
    row = lax.broadcasted_iota(jnp.int32, (16, SLICE), 0)
    pair = jnp.where(row == 0, high, jnp.where(row == 1, flat - high, 0.0))
    products = dot(pair.astype(jnp.bfloat16), query_in[...].reshape(N * 16, SLICE), NT)
    scores = products[0:1, :] + products[1:2, :]
    row = lax.broadcasted_iota(jnp.int32, (8, 128), 0)
    tile[...] = jnp.where(
        row == 0, scores[:, :128], jnp.where(row == 1, scores[:, 128:], squares)
    )

    to_add = exchange(
        NEAREST,
        lambda far: (z + 8 - far) % 8,
        lambda z, b: tile,
        tiles_in.at[my_slice],
        tile_send,
        tile_recv,
    )
    tiles_in[my_slice] = tile[...]
    for copy in sent + to_sum:
        copy.wait_send()
    for copy in to_add:
        copy.wait_recv()
    summed = jnp.sum(tiles_in[...], axis=0)
    norm = jnp.sqrt(summed[2:3, :] + 1e-06)
    out[:, :128] = summed[0:1, :] / norm
    out[:, 128:] = summed[1:2, :] / norm

    for copy in to_add:
        copy.wait_send()


def per_device(inputs, cotangent, gate_up, down_weight, proj_model, proj_hidden, lengths, queries):
    anywhere = pl.BlockSpec(memory_space=pl.ANY)
    bf16, f32 = jnp.bfloat16, jnp.float32
    dma = pltpu.SemaphoreType.DMA
    return pl.pallas_call(
        kernel,
        out_shape=jax.ShapeDtypeStruct((1, N * 16), f32),
        in_specs=[anywhere] * 8,
        out_specs=pl.BlockSpec(memory_space=pltpu.VMEM),
        scratch_shapes=[
            pltpu.VMEM((N, ROWS, WIDE), bf16),
            pltpu.VMEM((FF + RANK, D), bf16),
            pltpu.VMEM((2, N * ROWS, FF), bf16),
            pltpu.VMEM((N * ROWS, FF), f32),
            pltpu.VMEM((N * ROWS, FF), f32),
            pltpu.VMEM((ROWS, D), bf16),
            pltpu.VMEM((2 * RANK, D), bf16),
            pltpu.VMEM((3 * RANK, FF), bf16),
            pltpu.VMEM((N * ROWS, RANK), f32),
            pltpu.VMEM((4 * ROWS, FF + RANK), f32),
            pltpu.VMEM((3 * RANK, 4 * ROWS), f32),
            pltpu.VMEM((3 * RANK, RANK), f32),
            pltpu.VMEM((3 * RANK, 2 * RANK), f32),
            pltpu.VMEM((SLICES, 16, 128), f32),
            pltpu.VMEM((N, 16, 128), f32),
            pltpu.VMEM((2, 4, 2, 16, SLICE), bf16),
            pltpu.VMEM((8, 128), f32),
            pltpu.VMEM((SLICES, 8, 128), f32),
            pltpu.SMEM((1,), jnp.int32),
            dma((8 + PIECES,)),
            dma((N,)),
            dma((3, STEPS, PIECES)),
            dma((3, STEPS, PIECES)),
            dma((5,)),
            dma((5,)),
            dma((N,)),
            dma((N,)),
            dma((N,)),
            dma((N,)),
        ],
        compiler_params=pltpu.CompilerParams(
            collective_id=0, has_side_effects=True, vmem_limit_bytes=55091 * 1024
        ),
        cost_estimate=pl.CostEstimate(
            flops=4 * 10**9, bytes_accessed=12 * 10**6, transcendentals=10**6
        ),
    )(lengths, inputs, cotangent, gate_up, down_weight, proj_model.T, proj_hidden.T, queries)


def solution(mesh):
    return jax.shard_map(
        per_device,
        mesh=mesh,
        in_specs=(
            P(("dp", "tensor"), None),
            P(("dp", "tensor"), None),
            P(None, "dp", "tensor"),
            P("tensor", None),
            P(),
            P("tensor", None),
            P("dp"),
            P("dp", None),
        ),
        out_specs=P("dp", None),
        check_vma=False,
    )
```

```python
import jax
import jax.numpy as jnp
from jax import lax
from jax.experimental import pallas as pl
from jax.experimental.pallas import tpu as pltpu
from jax.sharding import PartitionSpec as P

MESH = pl.DeviceIdType.MESH
RANK = 64
N = 16
STEPS = 5
PIECES = 3
D = 4096
FF = 896
ROWS = 32
WIDE = D + 2 * RANK
SLICES = 8
SLICE = 1536
LINES = SLICE // 128
CUTS = ((0, 1408), (1408, 2816), (2816, D))
LEAD = CUTS[-1][0]
SHIFT = (0, 0, 2 * RANK)
NT = (((1,), (1,)), ((), ()))
OTHERS = [(4, 1), (4, 0)]
for far in (3, 2, 1):
    OTHERS += [(far, 1), (8 - far, 1), (far, 0), (8 - far, 0)]
OTHERS += [(0, 1)]
NEAREST = [(2, 1), (2, 0), (7, 1), (1, 1), (7, 0), (1, 0), (0, 1)]

DOWN, UP, ACROSS = 0, 1, 2


def span(piece):
    low, high = CUTS[piece]
    if piece == PIECES - 2:
        high += 2 * RANK
    return pl.ds(low + SHIFT[piece], high - low)


def slot_of(step, link):
    return 1 + 3 * (step - 1) + link


def dot(a, b, dims):
    return lax.dot_general(a, b, dims, preferred_element_type=jnp.float32)


def kernel(
    lengths,
    inputs,
    cotangent,
    gate_up,
    down_weight,
    proj_model,
    proj_hidden,
    queries,
    out,
    block,
    weight,
    gates,
    factor_up,
    factor_gate,
    x_rows,
    pm,
    ph,
    hidden_proj,
    grad,
    sources,
    total,
    turned,
    parts,
    parts_in,
    query_in,
    tile,
    tiles_in,
    length,
    load_sem,
    gate_sem,
    send_sem,
    recv_sem,
    query_send,
    query_recv,
    parts_send,
    parts_recv,
    tile_send,
    tile_recv,
):
    dp = lax.axis_index("dp")
    me = lax.axis_index("tensor")
    z, b = me // 2, me % 2
    z_down, z_up = (z + 7) % 8, (z + 1) % 8
    partner = me + 1 - 2 * b
    slice_of = lambda z, b: z % 4 * 2 + b
    my_slice = slice_of(z, b)
    target = {DOWN: z_up * 2 + b, UP: z_down * 2 + b, ACROSS: partner}

    y_hi, x, core = dp // 8, (dp // 2) % 4, dp % 2
    at = lambda y_hi, x, core: y_hi * 8 + x * 2 + core
    across = (at(1 - y_hi, x, core), partner)
    beside = (at(y_hi, x, 1 - core), me)
    x_up = (at(y_hi, (x + 1) % 4, core), me)
    x_down = (at(y_hi, (x + 3) % 4, core), me)

    owners = [me]
    same = lambda d: ((z + d + 8) % 8) * 2 + b
    opposite = lambda d: ((z + d + 8) % 8) * 2 + 1 - b
    for trio in (
        (same(-1), same(1), opposite(0)),
        (same(-2), same(2), opposite(1)),
        (same(-3), same(3), opposite(2)),
        (same(-4), opposite(3), opposite(-2)),
        (opposite(-3), opposite(4), opposite(-1)),
    ):
        owners += trio

    load_x = pltpu.make_async_copy(inputs, x_rows, load_sem.at[0])
    load_pm = pltpu.make_async_copy(proj_model.at[: 2 * RANK], pm, load_sem.at[1])
    load_last = pltpu.make_async_copy(
        proj_model.at[2 * RANK :], weight.at[FF:], load_sem.at[5 + PIECES]
    )
    load_own = [
        pltpu.make_async_copy(
            cotangent.at[:, pl.ds(low, high - low)],
            block.at[0, :, pl.ds(at, high - low)],
            load_sem.at[sem],
        )
        for low, high, at, sem in ((0, LEAD, 0, 2), (LEAD, D, LEAD + 2 * RANK, 7 + PIECES))
    ]
    load_ph = pltpu.make_async_copy(proj_hidden, ph, load_sem.at[3])
    load_query = pltpu.make_async_copy(
        queries.at[:, pl.ds(pl.multiple_of(my_slice * SLICE, 128), SLICE)],
        query_in.at[y_hi, x, core],
        load_sem.at[4],
    )
    load_weight = [
        pltpu.make_async_copy(
            down_weight.at[:, pl.ds(low, high - low)],
            weight.at[:FF, pl.ds(low, high - low)],
            load_sem.at[5 + j],
        )
        for j, (low, high) in enumerate(CUTS)
    ]
    load_gates = [
        pltpu.make_async_copy(
            gate_up.at[:, pl.ds(pl.multiple_of(owner * ROWS, ROWS), ROWS), :],
            gates.at[:, pl.ds(slot * ROWS, ROWS), :],
            gate_sem.at[slot],
        )
        for slot, owner in enumerate(owners)
    ]
    load_lengths = pltpu.make_async_copy(lengths, length, load_sem.at[6 + PIECES])

    barrier = pltpu.get_barrier_semaphore()
    for peer in [(dp, t) for t in target.values()] + [across, beside, x_up, x_down]:
        pl.semaphore_signal(barrier, inc=1, device_id=peer, device_id_type=MESH)
    load_x.start()
    load_pm.start()
    for copy in load_own:
        copy.start()
    pl.semaphore_wait(barrier, 7)

    def pass_on(step, link, piece, source=None):
        where = block.at[slot_of(step, link), :, span(piece)]
        return pltpu.make_async_remote_copy(
            src_ref=where if source is None else source,
            dst_ref=where,
            send_sem=send_sem.at[link, step - 1, piece],
            recv_sem=recv_sem.at[link, step - 1, piece],
            device_id=(dp, target[link]),
            device_id_type=MESH,
        )

    sent = []

    def send(step, link, piece, source_slot):
        copy = pass_on(step, link, piece, block.at[source_slot, :, span(piece)])
        copy.start()
        sent.append(copy)

    first_sends = [
        pass_on(1, link, piece, cotangent.at[:, span(piece)])
        for piece in range(PIECES - 2)
        for link in (DOWN, UP, ACROSS)
    ]
    sent += first_sends

    def send_first(turn):
        @pl.when(core == turn)
        def _():
            for copy in first_sends:
                copy.start()

    send_first(0)
    load_ph.start()
    load_lengths.start()
    for copy in load_gates:
        copy.start()
    load_last.start()
    for copy in load_weight:
        copy.start()
    load_query.start()
    load_x.wait()
    send_first(1)
    load_pm.wait()
    lead = dot(x_rows[...], pm[...], NT)
    for copy in load_own:
        copy.wait()
    block[0, :, LEAD : LEAD + 2 * RANK] = lead.astype(jnp.bfloat16)
    for piece in (PIECES - 2, PIECES - 1):
        for link in (DOWN, UP, ACROSS):
            send(1, link, piece, 0)

    def query_copy(source, slot, stage, peer):
        return pltpu.make_async_remote_copy(
            src_ref=source,
            dst_ref=query_in.at[slot],
            send_sem=query_send.at[stage],
            recv_sem=query_recv.at[stage],
            device_id=peer,
            device_id_type=MESH,
        )

    both = slice(None)
    x_before, x_after = (x + 3) % 4, (x + 1) % 4
    slots = [(y_hi, x, core), (both, x, core), (both, x), (both, x), (both, x_before)]
    arriving = [
        (1 - y_hi, x, core),
        (both, x, 1 - core),
        (both, x_before),
        (both, x_after),
        (both, (x + 2) % 4),
    ]
    peers = [across, beside, x_up, x_down, x_up]

    def send_queries(stage):
        if stage:
            source = query_in.at[slots[stage]]
        else:
            begin = pl.multiple_of(slice_of(z, 1 - b) * SLICE, 128)
            source = queries.at[:, pl.ds(begin, SLICE)]
        copy = query_copy(source, slots[stage], stage, peers[stage])
        copy.start()
        sent.append(copy)

    def wait_queries(stage):
        here = query_in.at[arriving[stage]]
        query_copy(here, arriving[stage], stage, peers[stage]).wait_recv()

    send_queries(0)

    load_ph.wait()

    def gate_rows(i, carry):
        rows = pl.ds(pl.multiple_of(i * ROWS, ROWS), ROWS)
        g = gates[0, rows, :].astype(jnp.float32)
        u = gates[1, rows, :].astype(jnp.float32)
        s = jax.nn.sigmoid(g)
        silu = g * s
        factor_up[rows, :] = silu
        factor_gate[rows, :] = u * s * (1.0 + g * (1.0 - s))
        hidden = (silu * u).astype(jnp.bfloat16)
        hidden_proj[rows, :] = dot(hidden, ph[2 * RANK :, :], NT)
        return carry

    total[...] = jnp.zeros_like(total)
    parts[...] = jnp.zeros_like(parts)
    load_lengths.wait()
    live_count = length[0]

    def multiply(first, count, piece):
        low, high = CUTS[piece]
        rows = count * ROWS
        at = low + SHIFT[piece]
        x = block[first : first + count, :, at : at + high - low].reshape(rows, high - low)
        for n in range(0, FF + RANK, 256):
            m = min(n + 256, FF + RANK)
            term = dot(x, weight[n:m, low:high], NT)
            if piece:
                term += grad[:rows, n:m]
            grad[:rows, n:m] = term

    def prepare(first, count):
        rows = count * ROWS
        here = pl.ds(first * ROWS, rows)
        lead = block[first : first + count, :, LEAD : LEAD + 2 * RANK].reshape(rows, 2 * RANK)
        row = lax.broadcasted_iota(jnp.int32, (ROWS, 3 * RANK), 0)
        live = jnp.concatenate(
            [
                (row + owners[slot] * ROWS < live_count).astype(jnp.float32)
                for slot in range(first, first + count)
            ],
            axis=0,
        )
        left = jnp.concatenate([lead.astype(jnp.float32), hidden_proj[here, :]], axis=1)
        sources[:, :rows] = (left * live).T

    def split(a):
        high = a.astype(jnp.bfloat16)
        return high, (a - high.astype(jnp.float32)).astype(jnp.bfloat16)

    def finish(first, count):
        rows = count * ROWS
        here = pl.ds(first * ROWS, rows)
        nn = (((1,), (0,)), ((), ()))
        source, source_low = split(sources[2 * RANK :, :rows])
        target, target_low = split(grad[:rows, FF:])
        last = dot(source, target, nn) + dot(source, target_low, nn)
        total[2 * RANK :, :] += last + dot(source_low, target, nn)
        for k, factor in enumerate((factor_gate, factor_up)):
            columns = slice(k * RANK, (k + 1) * RANK)
            moved = (grad[:rows, :FF] * factor[here, :]).astype(jnp.bfloat16)
            target, target_low = split(dot(moved, ph[columns, :], NT))
            source = sources[columns, :rows].astype(jnp.bfloat16)
            total[columns, :] += dot(source, target, nn) + dot(source, target_low, nn)

    onward = {
        (1, DOWN): [(2, DOWN, slot_of(1, DOWN))],
        (2, DOWN): [(3, DOWN, slot_of(2, DOWN))],
        (3, DOWN): [(4, DOWN, slot_of(3, DOWN))],
        (1, UP): [(2, UP, slot_of(1, UP)), (2, ACROSS, slot_of(1, UP))],
        (2, UP): [(3, UP, slot_of(2, UP)), (3, ACROSS, slot_of(2, UP))],
        (3, ACROSS): [(4, UP, slot_of(3, ACROSS)), (4, ACROSS, slot_of(2, DOWN))],
        (4, UP): [(5, UP, slot_of(4, UP))],
        (4, ACROSS): [(5, DOWN, slot_of(4, ACROSS)), (5, ACROSS, slot_of(1, DOWN))],
    }
    for step in range(1, STEPS + 1):
        first, count = (0, 4) if step == 1 else (slot_of(step, 0), 3)
        for piece in range(PIECES):
            for link in (ACROSS, UP, DOWN):
                pass_on(step, link, piece).wait_recv()
                for later, way, slot in onward.get((step, link), ()):
                    send(later, way, piece, slot)
            if step == 1:
                if not piece:
                    load_last.wait()
                load_weight[piece].wait()
            multiply(first, count, piece)
            if not piece:
                for slot in range(first, first + count):
                    load_gates[slot].wait()
                lax.fori_loop(first, first + count, gate_rows, 0)
            if piece == PIECES - 2:
                prepare(first, count)
        if step == 1:
            load_query.wait()
            wait_queries(0)
            send_queries(1)
        if step == 2:
            wait_queries(1)
            send_queries(2)
            send_queries(3)
        if step == 3:
            wait_queries(2)
            send_queries(4)
        if step == 4:
            wait_queries(3)
            wait_queries(4)
        finish(first, count)

    turned[: 3 * RANK, :] = jnp.concatenate([total[...], total[...]], axis=1)
    lane = lax.broadcasted_iota(jnp.int32, (LINES, 2 * RANK), 1)
    for i in range(SLICES):
        even = turned[pl.ds(2 * LINES * i, LINES, stride=2), :]
        odd = turned[pl.ds(2 * LINES * i + 1, LINES, stride=2), :]
        parts[i, :LINES, :] = jnp.where(lane < RANK, even, odd)

    def exchange(ways, peer_of, source, target, sends, recvs):
        copies = []
        for r, (far, over) in enumerate(ways):
            peer = (peer_of(far), 1 - b if over else b)
            copy = pltpu.make_async_remote_copy(
                src_ref=source(*peer),
                dst_ref=target,
                send_sem=sends.at[r],
                recv_sem=recvs.at[r],
                device_id=(dp, peer[0] * 2 + peer[1]),
                device_id_type=MESH,
            )
            copy.start()
            copies.append(copy)
        return copies

    to_sum = exchange(
        OTHERS,
        lambda far: (z + far) % 8,
        lambda z, b: parts.at[slice_of(z, b)],
        parts_in.at[me],
        parts_send,
        parts_recv,
    )
    parts_in[me] = parts[my_slice]
    for copy in to_sum:
        copy.wait_recv()

    entries = jnp.sum(parts_in[...], axis=0)
    squares = jnp.sum(entries * entries)
    flat = jnp.concatenate([entries[i : i + 1, :] for i in range(LINES)], axis=1)
    high = flat.astype(jnp.bfloat16).astype(jnp.float32)
    row = lax.broadcasted_iota(jnp.int32, (16, SLICE), 0)
    pair = jnp.where(row == 0, high, jnp.where(row == 1, flat - high, 0.0))
    products = dot(pair.astype(jnp.bfloat16), query_in[...].reshape(N * 16, SLICE), NT)
    scores = products[0:1, :] + products[1:2, :]
    row = lax.broadcasted_iota(jnp.int32, (8, 128), 0)
    tile[...] = jnp.where(
        row == 0, scores[:, :128], jnp.where(row == 1, scores[:, 128:], squares)
    )

    to_add = exchange(
        NEAREST,
        lambda far: (z + 8 - far) % 8,
        lambda z, b: tile,
        tiles_in.at[my_slice],
        tile_send,
        tile_recv,
    )
    tiles_in[my_slice] = tile[...]
    for copy in sent + to_sum:
        copy.wait_send()
    for copy in to_add:
        copy.wait_recv()
    summed = jnp.sum(tiles_in[...], axis=0)
    norm = jnp.sqrt(summed[2:3, :] + 1e-06)
    out[:, :128] = summed[0:1, :] / norm
    out[:, 128:] = summed[1:2, :] / norm

    for copy in to_add:
        copy.wait_send()


def per_device(inputs, cotangent, gate_up, down_weight, proj_model, proj_hidden, lengths, queries):
    anywhere = pl.BlockSpec(memory_space=pl.ANY)
    bf16, f32 = jnp.bfloat16, jnp.float32
    dma = pltpu.SemaphoreType.DMA
    return pl.pallas_call(
        kernel,
        out_shape=jax.ShapeDtypeStruct((1, N * 16), f32),
        in_specs=[anywhere] * 8,
        out_specs=pl.BlockSpec(memory_space=pltpu.VMEM),
        scratch_shapes=[
            pltpu.VMEM((N, ROWS, WIDE), bf16),
            pltpu.VMEM((FF + RANK, D), bf16),
            pltpu.VMEM((2, N * ROWS, FF), bf16),
            pltpu.VMEM((N * ROWS, FF), f32),
            pltpu.VMEM((N * ROWS, FF), f32),
            pltpu.VMEM((ROWS, D), bf16),
            pltpu.VMEM((2 * RANK, D), bf16),
            pltpu.VMEM((3 * RANK, FF), bf16),
            pltpu.VMEM((N * ROWS, RANK), f32),
            pltpu.VMEM((4 * ROWS, FF + RANK), f32),
            pltpu.VMEM((3 * RANK, 4 * ROWS), f32),
            pltpu.VMEM((3 * RANK, RANK), f32),
            pltpu.VMEM((3 * RANK + 8, 2 * RANK), f32),
            pltpu.VMEM((SLICES, 16, 128), f32),
            pltpu.VMEM((N, 16, 128), f32),
            pltpu.VMEM((2, 4, 2, 16, SLICE), bf16),
            pltpu.VMEM((8, 128), f32),
            pltpu.VMEM((SLICES, 8, 128), f32),
            pltpu.SMEM((1,), jnp.int32),
            dma((8 + PIECES,)),
            dma((N,)),
            dma((3, STEPS, PIECES)),
            dma((3, STEPS, PIECES)),
            dma((5,)),
            dma((5,)),
            dma((N,)),
            dma((N,)),
            dma((N,)),
            dma((N,)),
        ],
        compiler_params=pltpu.CompilerParams(
            collective_id=0, has_side_effects=True, vmem_limit_bytes=55091 * 1024
        ),
        cost_estimate=pl.CostEstimate(
            flops=4 * 10**9, bytes_accessed=12 * 10**6, transcendentals=10**6
        ),
    )(lengths, inputs, cotangent, gate_up, down_weight, proj_model.T, proj_hidden.T, queries)


def solution(mesh):
    return jax.shard_map(
        per_device,
        mesh=mesh,
        in_specs=(
            P(("dp", "tensor"), None),
            P(("dp", "tensor"), None),
            P(None, "dp", "tensor"),
            P("tensor", None),
            P(),
            P("tensor", None),
            P("dp"),
            P("dp", None),
        ),
        out_specs=P("dp", None),
        check_vma=False,
    )
```

```python
import jax
import jax.numpy as jnp
from jax import lax
from jax.experimental import pallas as pl
from jax.experimental.pallas import tpu as pltpu
from jax.sharding import PartitionSpec as P

MESH = pl.DeviceIdType.MESH
RANK = 64
N = 16
STEPS = 5
PIECES = 3
D = 4096
FF = 896
ROWS = 32
WIDE = D + 2 * RANK
SLICES = 8
SLICE = 1536
LINES = SLICE // 128
CUTS = ((0, 1408), (1408, 2816), (2816, D))
LEAD = CUTS[-1][0]
SHIFT = (0, 0, 2 * RANK)
NT = (((1,), (1,)), ((), ()))
OTHERS = [(4, 1), (4, 0)]
for far in (3, 2, 1):
    OTHERS += [(far, 1), (8 - far, 1), (far, 0), (8 - far, 0)]
OTHERS += [(0, 1)]
NEAREST = [(2, 1), (2, 0), (7, 1), (1, 1), (7, 0), (1, 0), (0, 1)]

DOWN, UP, ACROSS = 0, 1, 2


def span(piece):
    low, high = CUTS[piece]
    if piece == PIECES - 2:
        high += 2 * RANK
    return pl.ds(low + SHIFT[piece], high - low)


def slot_of(step, link):
    return 1 + 3 * (step - 1) + link


def dot(a, b, dims):
    return lax.dot_general(a, b, dims, preferred_element_type=jnp.float32)


def kernel(
    lengths,
    inputs,
    cotangent,
    gate_up,
    down_weight,
    proj_model,
    proj_hidden,
    queries,
    out,
    block,
    weight,
    gates,
    factor_up,
    factor_gate,
    x_rows,
    pm,
    ph,
    hidden_proj,
    grad,
    sources,
    total,
    turned,
    parts,
    parts_in,
    query_in,
    tile,
    tiles_in,
    length,
    load_sem,
    gate_sem,
    send_sem,
    recv_sem,
    query_send,
    query_recv,
    parts_send,
    parts_recv,
    tile_send,
    tile_recv,
):
    dp = lax.axis_index("dp")
    me = lax.axis_index("tensor")
    z, b = me // 2, me % 2
    z_down, z_up = (z + 7) % 8, (z + 1) % 8
    partner = me + 1 - 2 * b
    slice_of = lambda z, b: z % 4 * 2 + b
    my_slice = slice_of(z, b)
    target = {DOWN: z_up * 2 + b, UP: z_down * 2 + b, ACROSS: partner}

    y_hi, x, core = dp // 8, (dp // 2) % 4, dp % 2
    at = lambda y_hi, x, core: y_hi * 8 + x * 2 + core
    across = (at(1 - y_hi, x, core), partner)
    beside = (at(y_hi, x, 1 - core), me)
    x_up = (at(y_hi, (x + 1) % 4, core), me)
    x_down = (at(y_hi, (x + 3) % 4, core), me)

    owners = [me]
    same = lambda d: ((z + d + 8) % 8) * 2 + b
    opposite = lambda d: ((z + d + 8) % 8) * 2 + 1 - b
    for trio in (
        (same(-1), same(1), opposite(0)),
        (same(-2), same(2), opposite(1)),
        (same(-3), same(3), opposite(2)),
        (same(-4), opposite(3), opposite(-2)),
        (opposite(-3), opposite(4), opposite(-1)),
    ):
        owners += trio

    load_x = pltpu.make_async_copy(inputs, x_rows, load_sem.at[0])
    load_pm = pltpu.make_async_copy(proj_model.at[: 2 * RANK], pm, load_sem.at[1])
    load_last = pltpu.make_async_copy(
        proj_model.at[2 * RANK :], weight.at[FF:], load_sem.at[5 + PIECES]
    )
    load_own = [
        pltpu.make_async_copy(
            cotangent.at[:, pl.ds(low, high - low)],
            block.at[0, :, pl.ds(at, high - low)],
            load_sem.at[sem],
        )
        for low, high, at, sem in ((0, LEAD, 0, 2), (LEAD, D, LEAD + 2 * RANK, 7 + PIECES))
    ]
    load_ph = pltpu.make_async_copy(proj_hidden, ph, load_sem.at[3])
    load_query = pltpu.make_async_copy(
        queries.at[:, pl.ds(pl.multiple_of(my_slice * SLICE, 128), SLICE)],
        query_in.at[y_hi, x, core],
        load_sem.at[4],
    )
    load_weight = [
        pltpu.make_async_copy(
            down_weight.at[:, pl.ds(low, high - low)],
            weight.at[:FF, pl.ds(low, high - low)],
            load_sem.at[5 + j],
        )
        for j, (low, high) in enumerate(CUTS)
    ]
    load_gates = [
        pltpu.make_async_copy(
            gate_up.at[:, pl.ds(pl.multiple_of(owner * ROWS, ROWS), ROWS), :],
            gates.at[:, pl.ds(slot * ROWS, ROWS), :],
            gate_sem.at[slot],
        )
        for slot, owner in enumerate(owners)
    ]
    load_lengths = pltpu.make_async_copy(lengths, length, load_sem.at[6 + PIECES])

    barrier = pltpu.get_barrier_semaphore()
    for peer in [(dp, t) for t in target.values()] + [across, beside, x_up, x_down]:
        pl.semaphore_signal(barrier, inc=1, device_id=peer, device_id_type=MESH)
    load_x.start()
    load_pm.start()
    for copy in load_own:
        copy.start()
    pl.semaphore_wait(barrier, 7)

    def pass_on(step, link, piece, source=None):
        where = block.at[slot_of(step, link), :, span(piece)]
        return pltpu.make_async_remote_copy(
            src_ref=where if source is None else source,
            dst_ref=where,
            send_sem=send_sem.at[link, step - 1, piece],
            recv_sem=recv_sem.at[link, step - 1, piece],
            device_id=(dp, target[link]),
            device_id_type=MESH,
        )

    sent = []

    def send(step, link, piece, source_slot):
        copy = pass_on(step, link, piece, block.at[source_slot, :, span(piece)])
        copy.start()
        sent.append(copy)

    first_sends = [
        pass_on(1, link, piece, cotangent.at[:, span(piece)])
        for piece in range(PIECES - 2)
        for link in (DOWN, UP, ACROSS)
    ]
    sent += first_sends

    for copy in first_sends:
        copy.start()
    load_ph.start()
    load_lengths.start()
    for copy in load_gates:
        copy.start()
    load_last.start()
    for copy in load_weight:
        copy.start()
    load_query.start()
    load_x.wait()
    load_pm.wait()
    lead = dot(x_rows[...], pm[...], NT)
    for copy in load_own:
        copy.wait()
    block[0, :, LEAD : LEAD + 2 * RANK] = lead.astype(jnp.bfloat16)
    for piece in (PIECES - 2, PIECES - 1):
        for link in (DOWN, UP, ACROSS):
            send(1, link, piece, 0)

    def query_copy(source, slot, stage, peer):
        return pltpu.make_async_remote_copy(
            src_ref=source,
            dst_ref=query_in.at[slot],
            send_sem=query_send.at[stage],
            recv_sem=query_recv.at[stage],
            device_id=peer,
            device_id_type=MESH,
        )

    both = slice(None)
    x_before, x_after = (x + 3) % 4, (x + 1) % 4
    slots = [(y_hi, x, core), (both, x, core), (both, x), (both, x), (both, x_before)]
    arriving = [
        (1 - y_hi, x, core),
        (both, x, 1 - core),
        (both, x_before),
        (both, x_after),
        (both, (x + 2) % 4),
    ]
    peers = [across, beside, x_up, x_down, x_up]

    def send_queries(stage):
        if stage:
            source = query_in.at[slots[stage]]
        else:
            begin = pl.multiple_of(slice_of(z, 1 - b) * SLICE, 128)
            source = queries.at[:, pl.ds(begin, SLICE)]
        copy = query_copy(source, slots[stage], stage, peers[stage])
        copy.start()
        sent.append(copy)

    def wait_queries(stage):
        here = query_in.at[arriving[stage]]
        query_copy(here, arriving[stage], stage, peers[stage]).wait_recv()

    send_queries(0)

    load_ph.wait()

    def gate_rows(i, carry):
        rows = pl.ds(pl.multiple_of(i * ROWS, ROWS), ROWS)
        g = gates[0, rows, :].astype(jnp.float32)
        u = gates[1, rows, :].astype(jnp.float32)
        s = jax.nn.sigmoid(g)
        silu = g * s
        factor_up[rows, :] = silu
        factor_gate[rows, :] = u * s * (1.0 + g * (1.0 - s))
        hidden = (silu * u).astype(jnp.bfloat16)
        hidden_proj[rows, :] = dot(hidden, ph[2 * RANK :, :], NT)
        return carry

    total[...] = jnp.zeros_like(total)
    parts[...] = jnp.zeros_like(parts)
    load_lengths.wait()
    live_count = length[0]

    def multiply(first, count, piece):
        low, high = CUTS[piece]
        rows = count * ROWS
        at = low + SHIFT[piece]
        x = block[first : first + count, :, at : at + high - low].reshape(rows, high - low)
        for n in range(0, FF + RANK, 256):
            m = min(n + 256, FF + RANK)
            term = dot(x, weight[n:m, low:high], NT)
            if piece:
                term += grad[:rows, n:m]
            grad[:rows, n:m] = term

    def prepare(first, count):
        rows = count * ROWS
        here = pl.ds(first * ROWS, rows)
        lead = block[first : first + count, :, LEAD : LEAD + 2 * RANK].reshape(rows, 2 * RANK)
        row = lax.broadcasted_iota(jnp.int32, (ROWS, 3 * RANK), 0)
        live = jnp.concatenate(
            [
                (row + owners[slot] * ROWS < live_count).astype(jnp.float32)
                for slot in range(first, first + count)
            ],
            axis=0,
        )
        left = jnp.concatenate([lead.astype(jnp.float32), hidden_proj[here, :]], axis=1)
        sources[:, :rows] = (left * live).T

    def split(a):
        high = a.astype(jnp.bfloat16)
        return high, (a - high.astype(jnp.float32)).astype(jnp.bfloat16)

    def finish(first, count):
        rows = count * ROWS
        here = pl.ds(first * ROWS, rows)
        nn = (((1,), (0,)), ((), ()))
        source, source_low = split(sources[2 * RANK :, :rows])
        target, target_low = split(grad[:rows, FF:])
        last = dot(source, target, nn) + dot(source, target_low, nn)
        total[2 * RANK :, :] += last + dot(source_low, target, nn)
        for k, factor in enumerate((factor_gate, factor_up)):
            columns = slice(k * RANK, (k + 1) * RANK)
            moved = (grad[:rows, :FF] * factor[here, :]).astype(jnp.bfloat16)
            target, target_low = split(dot(moved, ph[columns, :], NT))
            source = sources[columns, :rows].astype(jnp.bfloat16)
            total[columns, :] += dot(source, target, nn) + dot(source, target_low, nn)

    onward = {
        (1, DOWN): [(2, DOWN, slot_of(1, DOWN))],
        (2, DOWN): [(3, DOWN, slot_of(2, DOWN))],
        (3, DOWN): [(4, DOWN, slot_of(3, DOWN))],
        (1, UP): [(2, UP, slot_of(1, UP)), (2, ACROSS, slot_of(1, UP))],
        (2, UP): [(3, UP, slot_of(2, UP)), (3, ACROSS, slot_of(2, UP))],
        (3, ACROSS): [(4, UP, slot_of(3, ACROSS)), (4, ACROSS, slot_of(2, DOWN))],
        (4, UP): [(5, UP, slot_of(4, UP))],
        (4, ACROSS): [(5, DOWN, slot_of(4, ACROSS)), (5, ACROSS, slot_of(1, DOWN))],
    }
    for step in range(1, STEPS + 1):
        first, count = (0, 4) if step == 1 else (slot_of(step, 0), 3)
        for piece in range(PIECES):
            for link in (ACROSS, UP, DOWN):
                pass_on(step, link, piece).wait_recv()
                for later, way, slot in onward.get((step, link), ()):
                    send(later, way, piece, slot)
            if step == 1:
                if not piece:
                    load_last.wait()
                load_weight[piece].wait()
            multiply(first, count, piece)
            if not piece:
                for slot in range(first, first + count):
                    load_gates[slot].wait()
                lax.fori_loop(first, first + count, gate_rows, 0)
            if piece == PIECES - 2:
                prepare(first, count)
        if step == 1:
            load_query.wait()
            wait_queries(0)
            send_queries(1)
        if step == 2:
            wait_queries(1)
            send_queries(2)
            send_queries(3)
        if step == 3:
            wait_queries(2)
            send_queries(4)
        if step == 4:
            wait_queries(3)
            wait_queries(4)
        finish(first, count)

    turned[: 3 * RANK, :] = jnp.concatenate([total[...], total[...]], axis=1)
    lane = lax.broadcasted_iota(jnp.int32, (LINES, 2 * RANK), 1)
    for i in range(SLICES):
        even = turned[pl.ds(2 * LINES * i, LINES, stride=2), :]
        odd = turned[pl.ds(2 * LINES * i + 1, LINES, stride=2), :]
        parts[i, :LINES, :] = jnp.where(lane < RANK, even, odd)

    def exchange(ways, peer_of, source, target, sends, recvs):
        copies = []
        for r, (far, over) in enumerate(ways):
            peer = (peer_of(far), 1 - b if over else b)
            copy = pltpu.make_async_remote_copy(
                src_ref=source(*peer),
                dst_ref=target,
                send_sem=sends.at[r],
                recv_sem=recvs.at[r],
                device_id=(dp, peer[0] * 2 + peer[1]),
                device_id_type=MESH,
            )
            copy.start()
            copies.append(copy)
        return copies

    to_sum = exchange(
        OTHERS,
        lambda far: (z + far) % 8,
        lambda z, b: parts.at[slice_of(z, b)],
        parts_in.at[me],
        parts_send,
        parts_recv,
    )
    parts_in[me] = parts[my_slice]
    for copy in to_sum:
        copy.wait_recv()

    entries = jnp.sum(parts_in[...], axis=0)
    squares = jnp.sum(entries * entries)
    flat = jnp.concatenate([entries[i : i + 1, :] for i in range(LINES)], axis=1)
    high = flat.astype(jnp.bfloat16).astype(jnp.float32)
    row = lax.broadcasted_iota(jnp.int32, (16, SLICE), 0)
    pair = jnp.where(row == 0, high, jnp.where(row == 1, flat - high, 0.0))
    products = dot(pair.astype(jnp.bfloat16), query_in[...].reshape(N * 16, SLICE), NT)
    scores = products[0:1, :] + products[1:2, :]
    row = lax.broadcasted_iota(jnp.int32, (8, 128), 0)
    tile[...] = jnp.where(
        row == 0, scores[:, :128], jnp.where(row == 1, scores[:, 128:], squares)
    )

    to_add = exchange(
        NEAREST,
        lambda far: (z + 8 - far) % 8,
        lambda z, b: tile,
        tiles_in.at[my_slice],
        tile_send,
        tile_recv,
    )
    tiles_in[my_slice] = tile[...]
    for copy in sent + to_sum:
        copy.wait_send()
    for copy in to_add:
        copy.wait_recv()
    summed = jnp.sum(tiles_in[...], axis=0)
    norm = jnp.sqrt(summed[2:3, :] + 1e-06)
    out[:, :128] = summed[0:1, :] / norm
    out[:, 128:] = summed[1:2, :] / norm

    for copy in to_add:
        copy.wait_send()


def per_device(inputs, cotangent, gate_up, down_weight, proj_model, proj_hidden, lengths, queries):
    anywhere = pl.BlockSpec(memory_space=pl.ANY)
    bf16, f32 = jnp.bfloat16, jnp.float32
    dma = pltpu.SemaphoreType.DMA
    return pl.pallas_call(
        kernel,
        out_shape=jax.ShapeDtypeStruct((1, N * 16), f32),
        in_specs=[anywhere] * 8,
        out_specs=pl.BlockSpec(memory_space=pltpu.VMEM),
        scratch_shapes=[
            pltpu.VMEM((N, ROWS, WIDE), bf16),
            pltpu.VMEM((FF + RANK, D), bf16),
            pltpu.VMEM((2, N * ROWS, FF), bf16),
            pltpu.VMEM((N * ROWS, FF), f32),
            pltpu.VMEM((N * ROWS, FF), f32),
            pltpu.VMEM((ROWS, D), bf16),
            pltpu.VMEM((2 * RANK, D), bf16),
            pltpu.VMEM((3 * RANK, FF), bf16),
            pltpu.VMEM((N * ROWS, RANK), f32),
            pltpu.VMEM((4 * ROWS, FF + RANK), f32),
            pltpu.VMEM((3 * RANK, 4 * ROWS), f32),
            pltpu.VMEM((3 * RANK, RANK), f32),
            pltpu.VMEM((3 * RANK + 8, 2 * RANK), f32),
            pltpu.VMEM((SLICES, 16, 128), f32),
            pltpu.VMEM((N, 16, 128), f32),
            pltpu.VMEM((2, 4, 2, 16, SLICE), bf16),
            pltpu.VMEM((8, 128), f32),
            pltpu.VMEM((SLICES, 8, 128), f32),
            pltpu.SMEM((1,), jnp.int32),
            dma((8 + PIECES,)),
            dma((N,)),
            dma((3, STEPS, PIECES)),
            dma((3, STEPS, PIECES)),
            dma((5,)),
            dma((5,)),
            dma((N,)),
            dma((N,)),
            dma((N,)),
            dma((N,)),
        ],
        compiler_params=pltpu.CompilerParams(
            collective_id=0, has_side_effects=True, vmem_limit_bytes=55091 * 1024
        ),
        cost_estimate=pl.CostEstimate(
            flops=4 * 10**9, bytes_accessed=12 * 10**6, transcendentals=10**6
        ),
    )(lengths, inputs, cotangent, gate_up, down_weight, proj_model.T, proj_hidden.T, queries)


def solution(mesh):
    return jax.shard_map(
        per_device,
        mesh=mesh,
        in_specs=(
            P(("dp", "tensor"), None),
            P(("dp", "tensor"), None),
            P(None, "dp", "tensor"),
            P("tensor", None),
            P(),
            P("tensor", None),
            P("dp"),
            P("dp", None),
        ),
        out_specs=P("dp", None),
        check_vma=False,
    )
```
